256 devices in a mesh: tgt: 16 (over z, y_lo), src: 16 (over x, y_hi, core).
Axes of the slice: x: 4, y: 4 (y_hi: 2, y_lo: 2; y = y_hi * 2 + y_lo), z: 8, core: 2. Of those that a mesh axis runs over, the one named last changes fastest.
Arguments:
- coefficients: bfloat16 [64, 16, 512, 512], P('tgt', 'src'), may hold values from -1.5 to 1.5
- factors: bfloat16 [3, 64, 16, 512, 512], P(None, 'tgt', 'src'), may hold values from -0.25 to 0.25
Outputs:
- potentials: float32 [64, 2, 256, 512], P('tgt', None, 'src')
The draws below stay inside these ranges and needn't reach their ends.
All inputs are finite; a program needn't handle non-finite values.
Results may differ from the reference program's by a relative error of at most 0.013.
Values may be sent and summed in bfloat16 or wider, within the bound.
No kernel may reach another device: no remote copies, remote signals or barrier semaphores. Data moves between devices by JAX's collectives and lax.ppermute only.
A program may use at most 64 MiB of HBM per device.

```python
import jax
import jax.numpy as jnp
from jax import lax

R = 256
RHS = 512
BLK = 4
LEVELS = 3
TBLOCKS = 64
N_TGT = 16
N_SRC = 16


def levels(own_key, extent, cuts, low, top_value):
    level, own = 1.0, jax.random.fold_in(own_key, 6)
    for dim, blocks in cuts:
        steps = jnp.exp(jax.random.uniform(jax.random.fold_in(own, dim), (blocks,), jnp.float32, low / len(cuts), top_value / len(cuts)))
        level = level * jnp.repeat(steps, extent[dim] // blocks).reshape([-1 if axis == dim else 1 for axis in range(len(extent))])
    return level


def centred(key, extent, spread, reach, pieces=(), kind=jnp.bfloat16):
    loudness = levels(key, extent, pieces, -0.22, 0.18) if pieces else 1.0
    result = jax.random.normal(key, extent, jnp.float32) * spread * loudness
    return jnp.minimum(jnp.maximum(result, -reach), reach).astype(kind)


def setup_inputs(seed: int = 0) -> dict:
    splits = jax.random.split(jax.random.key(seed), 3)
    return {
        "coefficients": centred(splits[0], (TBLOCKS, N_SRC, 2 * R, RHS), 0.25, 1.5, ((0, 16), (1, 16))),
        "factors": centred(splits[1], (LEVELS, TBLOCKS, N_SRC, 2 * R, 2 * R), (2 * R) ** -0.5, 0.25, ((1, 16), (2, 16))),
    }


def reference(coefficients, factors):
    total_blocks = coefficients.shape[0]
    bit_count = N_TGT.bit_length() - 1
    current = coefficients
    for section_index in range(LEVELS):
        def mix_block(block_index):
            weights = factors[section_index, block_index].astype(jnp.float32)
            block = current[block_index].astype(jnp.float32)
            return jnp.einsum('sij,sjn->sin', weights, block).astype(jnp.bfloat16)

        blended = lax.map(mix_block, jnp.arange(total_blocks, dtype=jnp.int32))
        shift = section_index % bit_count
        partner = jnp.bitwise_xor(jnp.arange(total_blocks, dtype=jnp.int32), jnp.int32(BLK << shift))
        lower = jnp.take(blended[:, :, R:], partner, axis=0)
        current = jnp.concatenate([blended[:, :, :R], lower], axis=2)
    summed = jnp.sum(current.astype(jnp.float32), axis=1)
    return summed.reshape(total_blocks, 2, R, summed.shape[-1])
```

```python
import functools

import jax
import jax.numpy as jnp
from jax import lax
from jax.experimental import pallas as pl
from jax.experimental.pallas import tpu as pltpu
from jax.sharding import PartitionSpec as P

AXES = ("tgt", "src")
BF = jnp.bfloat16
F32 = jnp.float32
WHOLE = pl.BlockSpec(memory_space=pltpu.VMEM)
SUMS = ((0, 1), (2,), (3,))


def moves(flip_tgt, flip_src, n_tgt, n_src):
    return [
        (t * n_src + s, (t ^ flip_tgt) * n_src + (s ^ flip_src))
        for t in range(n_tgt)
        for s in range(n_src)
    ]


def dot(a, b):
    return jnp.dot(a, b, preferred_element_type=F32)


def cost(flops, nbytes):
    return pl.CostEstimate(flops=flops, bytes_accessed=nbytes, transcendentals=0)


def first(factors, coefficients, blocks, part):
    rows, cols = coefficients.shape[2:]
    half = rows // 2
    lo, n = blocks

    def kernel(f_ref, c_ref, o_ref):
        o_ref[...] = dot(f_ref[...], c_ref[...]).astype(BF)

    return pl.pallas_call(
        kernel,
        grid=(n,),
        in_specs=[
            pl.BlockSpec((None, None, None, half, rows), lambda i: (0, lo + i, 0, part, 0)),
            pl.BlockSpec((None, None, rows, cols), lambda i: (lo + i, 0, 0, 0)),
        ],
        out_specs=pl.BlockSpec((None, half, cols), lambda i: (i, 0, 0)),
        out_shape=jax.ShapeDtypeStruct((n, half, cols), BF),
        cost_estimate=cost(2 * n * half * rows * cols, 2 * n * (half * rows + rows * cols)),
    )(factors, coefficients)


def middle(factors, up, got, b):
    half, cols = got.shape

    def kernel(f_ref, u_ref, g_ref, low_ref, up_ref):
        u, g = u_ref[...], g_ref[...]
        low_ref[...] = (dot(f_ref[half:, :half], u) + dot(f_ref[half:, half:], g)).astype(BF)
        up_ref[...] = (dot(f_ref[:half, :half], u) + dot(f_ref[:half, half:], g)).astype(BF)

    return pl.pallas_call(
        kernel,
        grid=(1,),
        in_specs=[
            pl.BlockSpec((None, None, None, 2 * half, 2 * half), lambda i: (1, b, 0, 0, 0)),
            WHOLE,
            WHOLE,
        ],
        out_specs=[WHOLE, WHOLE],
        out_shape=[jax.ShapeDtypeStruct((half, cols), BF)] * 2,
        cost_estimate=cost(8 * half * half * cols, 8 * half * half),
    )(factors, up, got)


def last(factors, up, got, b):
    half, cols = got.shape

    def kernel(f_ref, u_ref, g_ref, give_ref, keep_ref):
        even = lax.rem(lax.axis_index("src"), 2) == 0
        u, g = u_ref[...], g_ref[...]
        out = (dot(f_ref[:, :half], u) + dot(f_ref[:, half:], g)).astype(BF)
        for i in range(2 * half // 32):
            one, two = out[i * 32 : i * 32 + 16], out[i * 32 + 16 : i * 32 + 32]
            keep_ref[i * 16 : i * 16 + 16] = jnp.where(even, one, two)
            give_ref[i * 16 : i * 16 + 16] = jnp.where(even, two, one)

    return pl.pallas_call(
        kernel,
        grid=(1,),
        in_specs=[
            pl.BlockSpec((None, None, None, 2 * half, 2 * half), lambda i: (2, b, 0, 0, 0)),
            WHOLE,
            WHOLE,
        ],
        out_specs=[WHOLE, WHOLE],
        out_shape=[jax.ShapeDtypeStruct((half, cols), BF)] * 2,
        cost_estimate=cost(8 * half * half * cols, 8 * half * half),
    )(factors, up, got)


def solution(mesh):
    n_tgt, n_src = mesh.shape["tgt"], mesh.shape["src"]

    def swap(v, flip_tgt, flip_src):
        return lax.ppermute(v, AXES, moves(flip_tgt, flip_src, n_tgt, n_src))

    def local(coefficients, factors):
        blocks, _, rows, cols = coefficients.shape
        half = rows // 2
        me = lax.axis_index("src")
        x, yh = me // 4, (me // 2) % 2
        up, got = [], []
        for b in range(blocks):
            got.append(swap(first(factors, coefficients, (b, 1), 1)[0], 1, 0))
        upper = first(factors, coefficients, (0, blocks), 0)
        for b in range(blocks):
            low, now = middle(factors, upper[b], got[b], b)
            up.append(now)
            got[b] = swap(low, 2, 0)
        pairs = []
        for b in range(blocks):
            give, keep = last(factors, up[b], got[b], b)
            pairs.append((keep.astype(F32) + swap(give, 0, 1).astype(F32)).astype(BF).reshape(2, 4, 2, 16, cols))
        totals = []
        for group in SUMS:
            pair = jnp.stack([pairs[b] for b in group])
            total = lax.dynamic_index_in_dim(pair, x, 2, False).astype(F32)
            for d in (1, 3, 2):
                part = lax.dynamic_index_in_dim(pair, x ^ d, 2, False)
                total = total + swap(part, 0, d * 4).astype(F32)
            totals.append(total.astype(BF))
        total = jnp.concatenate(totals)
        mine = lax.dynamic_index_in_dim(total, yh, 2, False)
        other = lax.dynamic_index_in_dim(total, 1 - yh, 2, False)
        upper = mine[:, 0].astype(F32) + swap(other[:, 0], 0, 2).astype(F32)
        lower = swap(mine[:, 1], 4, 0).astype(F32) + swap(other[:, 1], 4, 2).astype(F32)
        return jnp.stack([upper, lower], axis=1)

    return jax.shard_map(
        local,
        mesh=mesh,
        in_specs=(P("tgt", "src", None, None), P(None, "tgt", "src", None, None)),
        out_specs=P("tgt", None, "src", None),
        check_vma=False,
    )
```

```python
import jax
import jax.numpy as jnp
from jax import lax
from jax.experimental import pallas as pl
from jax.experimental.pallas import tpu as pltpu
from jax.sharding import PartitionSpec as P

AXES = ("tgt", "src")
BF = jnp.bfloat16
F32 = jnp.float32
VMEM = pl.BlockSpec(memory_space=pltpu.VMEM)
ANY = pl.BlockSpec(memory_space=pl.ANY)
SMALL = pltpu.CompilerParams(vmem_limit_bytes=12 << 20)
LARGE = pltpu.CompilerParams(vmem_limit_bytes=58 << 20)


def moves(flip_tgt, flip_src, n_tgt, n_src):
    return [
        (t * n_src + s, (t ^ flip_tgt) * n_src + (s ^ flip_src))
        for t in range(n_tgt)
        for s in range(n_src)
    ]


def dot(a, b):
    return jnp.dot(a, b, preferred_element_type=F32)


def opening(factors, coefficients):
    _, _, rows, cols = coefficients.shape
    half = rows // 2

    def kernel(f_hbm, c_hbm, o_ref, f_ref, c_ref, sems):
        copies = [
            pltpu.make_async_copy(f_hbm.at[0, 0, 0, pl.ds(half, half)], f_ref, sems.at[0]),
            pltpu.make_async_copy(c_hbm.at[0, 0], c_ref, sems.at[1]),
        ]
        for copy in copies:
            copy.start()
        for copy in copies:
            copy.wait()
        o_ref[...] = dot(f_ref[...], c_ref[...]).astype(BF)

    return pl.pallas_call(
        kernel,
        in_specs=[ANY, ANY],
        out_specs=VMEM,
        out_shape=jax.ShapeDtypeStruct((half, cols), BF),
        scratch_shapes=[
            pltpu.VMEM((half, rows), BF),
            pltpu.VMEM((rows, cols), BF),
            pltpu.SemaphoreType.DMA((2,)),
        ],
        compiler_params=LARGE,
        name="opening",
    )(factors, coefficients)


def lower(factors, coefficients, after):
    blocks, _, rows, cols = coefficients.shape
    half = rows // 2

    def kernel(f_hbm, c_hbm, _, *refs):
        outs, (f_ref, c_ref, sems) = refs[: blocks - 1], refs[blocks - 1 :]
        copies = [
            (
                pltpu.make_async_copy(f_hbm.at[0, b, 0, pl.ds(half, half)], f_ref.at[b - 1], sems.at[0, b - 1]),
                pltpu.make_async_copy(c_hbm.at[b, 0], c_ref.at[b - 1], sems.at[1, b - 1]),
            )
            for b in range(1, blocks)
        ]
        for pair in copies:
            for copy in pair:
                copy.start()
        for b, pair in enumerate(copies):
            for copy in pair:
                copy.wait()
            outs[b][...] = dot(f_ref[b], c_ref[b]).astype(BF)

    return pl.pallas_call(
        kernel,
        in_specs=[ANY] * 3,
        out_specs=[VMEM] * (blocks - 1),
        out_shape=[jax.ShapeDtypeStruct((half, cols), BF)] * (blocks - 1),
        scratch_shapes=[
            pltpu.VMEM((blocks - 1, half, rows), BF),
            pltpu.VMEM((blocks - 1, rows, cols), BF),
            pltpu.SemaphoreType.DMA((2, blocks - 1)),
        ],
        compiler_params=LARGE,
        name="lower",
    )(factors, coefficients, after)


def upper(factors, coefficients, after):
    levels, blocks = factors.shape[:2]
    _, _, rows, cols = coefficients.shape
    half = rows // 2

    def kernel(f_hbm, c_hbm, _, *refs):
        outs, later, (f_ref, c_ref, sems) = refs[:blocks], refs[blocks : blocks + levels - 1], refs[blocks + levels - 1 :]
        copies = [
            (
                pltpu.make_async_copy(f_hbm.at[0, b, 0, pl.ds(0, half)], f_ref.at[b], sems.at[0, b]),
                pltpu.make_async_copy(c_hbm.at[b, 0], c_ref.at[b], sems.at[1, b]),
            )
            for b in range(blocks)
        ]
        ahead = [
            pltpu.make_async_copy(f_hbm.at[level, :, 0], later[level - 1], sems.at[2, level])
            for level in range(1, levels)
        ]
        for pair in copies:
            for copy in pair:
                copy.start()
        for copy in ahead:
            copy.start()
        for b, pair in enumerate(copies):
            for copy in pair:
                copy.wait()
            outs[b][...] = dot(f_ref[b], c_ref[b]).astype(BF)
        for copy in ahead:
            copy.wait()

    return pl.pallas_call(
        kernel,
        in_specs=[ANY] * 3,
        out_specs=[VMEM] * (blocks + levels - 1),
        out_shape=[jax.ShapeDtypeStruct((half, cols), BF)] * blocks
        + [jax.ShapeDtypeStruct((blocks, rows, rows), BF)] * (levels - 1),
        scratch_shapes=[
            pltpu.VMEM((blocks, half, rows), BF),
            pltpu.VMEM((blocks, rows, cols), BF),
            pltpu.SemaphoreType.DMA((3, blocks)),
        ],
        compiler_params=SMALL,
        name="upper",
    )(factors, coefficients, after)


def middle(weights, up, got, b, *after):
    half, cols = got.shape

    def kernel(f_ref, u_ref, g_ref, *refs):
        low_ref, up_ref = refs[len(after) :]
        w = f_ref.at[b]
        u, g = u_ref[...], g_ref[...]
        low_ref[...] = (dot(w[half:, :half], u) + dot(w[half:, half:], g)).astype(BF)
        up_ref[...] = (dot(w[:half, :half], u) + dot(w[:half, half:], g)).astype(BF)

    return pl.pallas_call(
        kernel,
        in_specs=[VMEM] * (3 + len(after)),
        out_specs=[VMEM, VMEM],
        out_shape=[jax.ShapeDtypeStruct((half, cols), BF)] * 2,
        compiler_params=SMALL,
        name=f"middle{b}",
    )(weights, up, got, *after)


def last(weights, up, got, b, *after):
    half, cols = got.shape

    def kernel(f_ref, u_ref, g_ref, *refs):
        give_ref, keep_ref = refs[len(after) :]
        even = lax.rem(lax.axis_index("src"), 2) == 0
        w = f_ref.at[b]
        u, g = u_ref[...], g_ref[...]
        out = (dot(w[:, :half], u) + dot(w[:, half:], g)).astype(BF)
        for i in range(2 * half // 32):
            one, two = out[i * 32 : i * 32 + 16], out[i * 32 + 16 : i * 32 + 32]
            keep_ref[i * 16 : i * 16 + 16] = jnp.where(even, one, two)
            give_ref[i * 16 : i * 16 + 16] = jnp.where(even, two, one)

    return pl.pallas_call(
        kernel,
        in_specs=[VMEM] * (3 + len(after)),
        out_specs=[VMEM, VMEM],
        out_shape=[jax.ShapeDtypeStruct((half, cols), BF)] * 2,
        compiler_params=SMALL,
        name=f"last{b}",
    )(weights, up, got, *after)


def solution(mesh):
    n_tgt, n_src = mesh.shape["tgt"], mesh.shape["src"]

    def swap(v, flip_tgt, flip_src):
        return lax.ppermute(v, AXES, moves(flip_tgt, flip_src, n_tgt, n_src))

    def add(a, b):
        return a.astype(F32) + b.astype(F32)

    def pick(v, i):
        return lax.dynamic_index_in_dim(v, i, 1, False)

    def local(coefficients, factors):
        blocks, _, rows, cols = coefficients.shape
        me = lax.axis_index("src")
        x, yh = me // 4, (me // 2) % 2
        low = [opening(factors, coefficients)]
        low += lower(factors, coefficients, low[0])
        got = [swap(v, 1, 0) for v in low]
        *up, second, third = upper(factors, coefficients, low[-1])
        pairs, halves, totals = [None] * blocks, [None] * blocks, [None] * blocks
        order = second

        def mix(b, *after):
            nonlocal order
            order, up[b] = middle(second, up[b], got[b], b, order, *after)
            got[b] = swap(order, 2, 0)

        def end(b, *after):
            nonlocal order
            order, keep = last(third, up[b], got[b], b, order, *after)
            pairs[b] = add(keep, swap(order, 0, 1)).astype(BF).reshape(2, 4, 2, 16, cols)

        def halve(b):
            pair = pairs[b]
            back = swap(jnp.stack([pick(pair, x ^ 1), pick(pair, x ^ 2)]), 0, 4)
            halves[b] = add(jnp.stack([pick(pair, x), pick(pair, x ^ 3)]), back).astype(BF)

        def quarter(b):
            totals[b] = add(halves[b][0], swap(halves[b][1], 0, 12)).astype(BF)

        mix(0)
        mix(1)
        end(0)
        mix(2, pairs[0])
        halve(0)
        end(1)
        mix(3, pairs[1], halves[0])
        halve(1)
        quarter(0)
        end(2)
        end(3, pairs[2], halves[1], totals[0])
        halve(2)
        quarter(1)
        quarter(2)
        total = pick(pairs[3], x).astype(F32)
        for d in (1, 3, 2):
            total = total + swap(pick(pairs[3], x ^ d), 0, d * 4).astype(F32)
        totals[3] = total.astype(BF)
        total = jnp.stack(totals, axis=2)
        mine, other = pick(total, yh), pick(total, 1 - yh)
        lows = add(swap(other[1], 4, 2), swap(mine[1], 4, 0))
        ups = add(mine[0], swap(other[0], 0, 2))
        return jnp.stack([ups, lows], axis=1)

    return jax.shard_map(
        local,
        mesh=mesh,
        in_specs=(P("tgt", "src", None, None), P(None, "tgt", "src", None, None)),
        out_specs=P("tgt", None, "src", None),
        check_vma=False,
    )
```

```python
import jax
import jax.numpy as jnp
from jax import lax
from jax.experimental import pallas as pl
from jax.experimental.pallas import tpu as pltpu
from jax.sharding import PartitionSpec as P

AXES = ("tgt", "src")
BF = jnp.bfloat16
F32 = jnp.float32
VMEM = pl.BlockSpec(memory_space=pltpu.VMEM)
ANY = pl.BlockSpec(memory_space=pl.ANY)
SMALL = pltpu.CompilerParams(vmem_limit_bytes=12 << 20)
ZP, AP = 1, 1
LARGE = pltpu.CompilerParams(vmem_limit_bytes=58 << 20)


def moves(flip_tgt, flip_src, n_tgt, n_src):
    return [
        (t * n_src + s, (t ^ flip_tgt) * n_src + (s ^ flip_src))
        for t in range(n_tgt)
        for s in range(n_src)
    ]


def dot(a, b):
    return jnp.dot(a, b, preferred_element_type=F32)


def opening(factors, coefficients):
    _, _, rows, cols = coefficients.shape
    half = rows // 2

    def kernel(f_hbm, c_hbm, o_ref, f_ref, c_ref, sems):
        copies = [
            pltpu.make_async_copy(f_hbm.at[0, 0, 0, pl.ds(half, half)], f_ref, sems.at[0]),
            pltpu.make_async_copy(c_hbm.at[0, 0], c_ref, sems.at[1]),
        ]
        for copy in copies:
            copy.start()
        for copy in copies:
            copy.wait()
        o_ref[...] = dot(f_ref[...], c_ref[...]).astype(BF)

    return pl.pallas_call(
        kernel,
        in_specs=[ANY, ANY],
        out_specs=VMEM,
        out_shape=jax.ShapeDtypeStruct((half, cols), BF),
        scratch_shapes=[
            pltpu.VMEM((half, rows), BF),
            pltpu.VMEM((rows, cols), BF),
            pltpu.SemaphoreType.DMA((2,)),
        ],
        compiler_params=LARGE,
        name="opening",
    )(factors, coefficients)


def lower(factors, coefficients, after):
    blocks, _, rows, cols = coefficients.shape
    half = rows // 2

    def kernel(f_hbm, c_hbm, _, *refs):
        outs, (f_ref, c_ref, sems) = refs[: blocks - 1], refs[blocks - 1 :]
        copies = [
            (
                pltpu.make_async_copy(f_hbm.at[0, b, 0, pl.ds(half, half)], f_ref.at[b - 1], sems.at[0, b - 1]),
                pltpu.make_async_copy(c_hbm.at[b, 0], c_ref.at[b - 1], sems.at[1, b - 1]),
            )
            for b in range(1, blocks)
        ]
        for pair in copies:
            for copy in pair:
                copy.start()
        for b, pair in enumerate(copies):
            for copy in pair:
                copy.wait()
            outs[b][...] = dot(f_ref[b], c_ref[b]).astype(BF)

    return pl.pallas_call(
        kernel,
        in_specs=[ANY] * 3,
        out_specs=[VMEM] * (blocks - 1),
        out_shape=[jax.ShapeDtypeStruct((half, cols), BF)] * (blocks - 1),
        scratch_shapes=[
            pltpu.VMEM((blocks - 1, half, rows), BF),
            pltpu.VMEM((blocks - 1, rows, cols), BF),
            pltpu.SemaphoreType.DMA((2, blocks - 1)),
        ],
        compiler_params=LARGE,
        name="lower",
    )(factors, coefficients, after)


def upper(factors, coefficients, after):
    blocks, _, rows, cols = coefficients.shape
    half = rows // 2

    def kernel(f_hbm, c_hbm, _, *refs):
        outs, (f_ref, c_ref, sems) = refs[:blocks], refs[blocks:]
        copies = [
            (
                pltpu.make_async_copy(f_hbm.at[0, b, 0, pl.ds(0, half)], f_ref.at[b], sems.at[0, b]),
                pltpu.make_async_copy(c_hbm.at[b, 0], c_ref.at[b], sems.at[1, b]),
            )
            for b in range(blocks)
        ]
        for pair in copies:
            for copy in pair:
                copy.start()
        for b, pair in enumerate(copies):
            for copy in pair:
                copy.wait()
            outs[b][...] = dot(f_ref[b], c_ref[b]).astype(BF)

    return pl.pallas_call(
        kernel,
        in_specs=[ANY] * 3,
        out_specs=[VMEM] * blocks,
        out_shape=[jax.ShapeDtypeStruct((half, cols), BF)] * blocks,
        scratch_shapes=[
            pltpu.VMEM((blocks, half, rows), BF),
            pltpu.VMEM((blocks, rows, cols), BF),
            pltpu.SemaphoreType.DMA((2, blocks)),
        ],
        compiler_params=LARGE,
        name="upper",
    )(factors, coefficients, after)


def middle(factors, up, got, b, *after):
    half, cols = got.shape

    def kernel(f_ref, u_ref, g_ref, *refs):
        low_ref, up_ref = refs[len(after) :]
        w = f_ref.at[1, b, 0]
        u, g = u_ref[...], g_ref[...]
        low_ref[...] = (dot(w[half:, :half], u) + dot(w[half:, half:], g)).astype(BF)
        up_ref[...] = (dot(w[:half, :half], u) + dot(w[:half, half:], g)).astype(BF)

    return pl.pallas_call(
        kernel,
        in_specs=[VMEM] * (3 + len(after)),
        out_specs=[VMEM, VMEM],
        out_shape=[jax.ShapeDtypeStruct((half, cols), BF)] * 2,
        compiler_params=SMALL,
        name=f"middle{b}",
    )(factors, up, got, *after)


def last(factors, up, got, b, *after):
    half, cols = got.shape

    def kernel(f_ref, u_ref, g_ref, *refs):
        give_ref, keep_ref = refs[len(after) :]
        even = lax.rem(lax.axis_index("src"), 2) == 0
        w = f_ref.at[2, b, 0]
        u, g = u_ref[...], g_ref[...]
        out = (dot(w[:, :half], u) + dot(w[:, half:], g)).astype(BF)
        for i in range(2 * half // 32):
            one, two = out[i * 32 : i * 32 + 16], out[i * 32 + 16 : i * 32 + 32]
            keep_ref[i * 16 : i * 16 + 16] = jnp.where(even, one, two)
            give_ref[i * 16 : i * 16 + 16] = jnp.where(even, two, one)

    return pl.pallas_call(
        kernel,
        in_specs=[VMEM] * (3 + len(after)),
        out_specs=[VMEM, VMEM],
        out_shape=[jax.ShapeDtypeStruct((half, cols), BF)] * 2,
        compiler_params=SMALL,
        name=f"last{b}",
    )(factors, up, got, *after)


def solution(mesh):
    n_tgt, n_src = mesh.shape["tgt"], mesh.shape["src"]

    def swap(v, flip_tgt, flip_src):
        return lax.ppermute(v, AXES, moves(flip_tgt, flip_src, n_tgt, n_src))

    def pieces(v, n, flip_tgt, flip_src):
        step = v.shape[0] // n
        return jnp.concatenate(
            [swap(v[i * step : (i + 1) * step], flip_tgt, flip_src) for i in range(n)]
        )

    def add(a, b):
        return a.astype(F32) + b.astype(F32)

    def pick(v, i):
        return lax.dynamic_index_in_dim(v, i, 1, False)

    def local(coefficients, factors):
        blocks, _, rows, cols = coefficients.shape
        me = lax.axis_index("src")
        x, yh = me // 4, (me // 2) % 2
        low = [opening(factors, coefficients)]
        low += lower(factors, coefficients, low[0])
        got = [swap(v, 1, 0) for v in low]
        up = list(upper(factors, coefficients, low[-1]))
        pairs, halves, totals = [None] * blocks, [None] * blocks, [None] * blocks
        order = up[0]

        def mix(b, *after):
            nonlocal order
            order, up[b] = middle(factors, up[b], got[b], b, order, *after)
            got[b] = pieces(order, ZP, 2, 0)

        def end(b, *after):
            nonlocal order
            order, keep = last(factors, up[b], got[b], b, order, *after)
            pairs[b] = add(keep, pieces(order, AP, 0, 1)).astype(BF).reshape(2, 4, 2, 16, cols)

        def halve(b, near):
            pair, far = pairs[b], 4 - near
            back = swap(jnp.stack([pick(pair, x ^ near), pick(pair, x ^ 2)]), 0, near * 4)
            halves[b] = add(jnp.stack([pick(pair, x), pick(pair, x ^ far)]), back).astype(BF)

        def quarter(b, near):
            totals[b] = add(halves[b][0], swap(halves[b][1], 0, (4 - near) * 4)).astype(BF)

        def direct(*group):
            pair = jnp.stack([pairs[b] for b in group], axis=3)
            total = pick(pair, x).astype(F32)
            for d in (1, 3, 2):
                total = total + swap(pick(pair, x ^ d), 0, d * 4).astype(F32)
            for i, b in enumerate(group):
                totals[b] = total[:, :, i].astype(BF)

        mix(0)
        mix(1)
        mix(2)
        end(0)
        mix(3)
        end(1)
        halve(0, 1)
        halve(1, 3)
        quarter(0, 1)
        end(2)
        end(3)
        halve(2, 1)
        quarter(1, 3)
        quarter(2, 1)
        direct(3)
        total = jnp.stack(totals, axis=2)
        mine, other = pick(total, yh), pick(total, 1 - yh)
        lows = add(swap(other[1], 4, 2), swap(mine[1], 4, 0))
        ups = add(mine[0], swap(other[0], 0, 2))
        return jnp.stack([ups, lows], axis=1)

    return jax.shard_map(
        local,
        mesh=mesh,
        in_specs=(P("tgt", "src", None, None), P(None, "tgt", "src", None, None)),
        out_specs=P("tgt", None, "src", None),
        check_vma=False,
    )
```

```python
import jax
import jax.numpy as jnp
from jax import lax
from jax.experimental import pallas as pl
from jax.experimental.pallas import tpu as pltpu
from jax.sharding import PartitionSpec as P

AXES = ("tgt", "src")
BF = jnp.bfloat16
F32 = jnp.float32
VMEM = pl.BlockSpec(memory_space=pltpu.VMEM)
ANY = pl.BlockSpec(memory_space=pl.ANY)
SMALL = pltpu.CompilerParams(vmem_limit_bytes=12 << 20)
ZP, AP = 1, 2
LARGE = pltpu.CompilerParams(vmem_limit_bytes=58 << 20)


def moves(flip_tgt, flip_src, n_tgt, n_src):
    return [
        (t * n_src + s, (t ^ flip_tgt) * n_src + (s ^ flip_src))
        for t in range(n_tgt)
        for s in range(n_src)
    ]


def dot(a, b):
    return jnp.dot(a, b, preferred_element_type=F32)


def opening(factors, coefficients):
    _, _, rows, cols = coefficients.shape
    half = rows // 2

    def kernel(f_hbm, c_hbm, o_ref, token_ref, f_ref, c_ref, sems):
        copies = [
            pltpu.make_async_copy(f_hbm.at[0, 0, 0, pl.ds(half, half)], f_ref, sems.at[0]),
            pltpu.make_async_copy(c_hbm.at[0, 0], c_ref, sems.at[1]),
        ]
        for copy in copies:
            copy.start()
        for copy in copies:
            copy.wait()
        o_ref[...] = dot(f_ref[...], c_ref[...]).astype(BF)
        token_ref[...] = c_ref[:16, :128]

    return pl.pallas_call(
        kernel,
        in_specs=[ANY, ANY],
        out_specs=[VMEM, VMEM],
        out_shape=[jax.ShapeDtypeStruct((half, cols), BF), jax.ShapeDtypeStruct((16, 128), BF)],
        scratch_shapes=[
            pltpu.VMEM((half, rows), BF),
            pltpu.VMEM((rows, cols), BF),
            pltpu.SemaphoreType.DMA((2,)),
        ],
        compiler_params=LARGE,
        name="opening",
    )(factors, coefficients)


def first(factors, coefficients, blocks, below, *after):
    _, _, rows, cols = coefficients.shape
    half = rows // 2
    top = half if below else 0

    def kernel(f_ref, c_ref, *refs):
        for b, out in zip(blocks, refs[len(after) :]):
            out[...] = dot(f_ref[0, b, 0, top : top + half], c_ref[b, 0]).astype(BF)

    return pl.pallas_call(
        kernel,
        in_specs=[VMEM] * (2 + len(after)),
        out_specs=[VMEM] * len(blocks),
        out_shape=[jax.ShapeDtypeStruct((half, cols), BF)] * len(blocks),
        compiler_params=SMALL,
        name="lower" if below else "upper",
    )(factors, coefficients, *after)


def rest(factors, coefficients, after):
    blocks, _, rows, cols = coefficients.shape
    half = rows // 2

    def kernel(f_ref, c_ref, _, *refs):
        outs, later, sems = refs[:blocks], refs[blocks:-1], refs[-1]
        copies = [
            pltpu.make_async_copy(f_ref.at[1 + i // blocks, i % blocks, 0], later[i], sems.at[i])
            for i in range(2 * blocks)
        ]
        for copy in copies:
            copy.start()
        for b, out in enumerate(outs):
            out[...] = dot(f_ref[0, b, 0, :half], c_ref[b, 0]).astype(BF)
        for copy in copies:
            copy.wait()

    out = pl.pallas_call(
        kernel,
        in_specs=[VMEM] * 3,
        out_specs=[VMEM] * 3 * blocks,
        out_shape=[jax.ShapeDtypeStruct((half, cols), BF)] * blocks
        + [jax.ShapeDtypeStruct((rows, rows), BF)] * (2 * blocks),
        scratch_shapes=[pltpu.SemaphoreType.DMA((2 * blocks,))],
        compiler_params=SMALL,
        name="upper",
    )(factors, coefficients, after)
    return list(out[:blocks]), out[blocks : 2 * blocks], out[2 * blocks :]


def middle(weights, up, got, b, *after):
    half, cols = got.shape

    def kernel(f_ref, u_ref, g_ref, *refs):
        low_ref, up_ref = refs[len(after) :]
        w = f_ref
        u, g = u_ref[...], g_ref[...]
        low_ref[...] = (dot(w[half:, :half], u) + dot(w[half:, half:], g)).astype(BF)
        up_ref[...] = (dot(w[:half, :half], u) + dot(w[:half, half:], g)).astype(BF)

    return pl.pallas_call(
        kernel,
        in_specs=[VMEM] * (3 + len(after)),
        out_specs=[VMEM, VMEM],
        out_shape=[jax.ShapeDtypeStruct((half, cols), BF)] * 2,
        compiler_params=SMALL,
        name=f"middle{b}",
    )(weights, up, got, *after)


def last(weights, up, got, b, *after):
    half, cols = got.shape

    def kernel(f_ref, u_ref, g_ref, *refs):
        give_ref, keep_ref = refs[len(after) :]
        even = lax.rem(lax.axis_index("src"), 2) == 0
        w = f_ref
        u, g = u_ref[...], g_ref[...]
        out = (dot(w[:, :half], u) + dot(w[:, half:], g)).astype(BF)
        for i in range(2 * half // 32):
            one, two = out[i * 32 : i * 32 + 16], out[i * 32 + 16 : i * 32 + 32]
            keep_ref[i * 16 : i * 16 + 16] = jnp.where(even, one, two)
            give_ref[i * 16 : i * 16 + 16] = jnp.where(even, two, one)

    return pl.pallas_call(
        kernel,
        in_specs=[VMEM] * (3 + len(after)),
        out_specs=[VMEM, VMEM],
        out_shape=[jax.ShapeDtypeStruct((half, cols), BF)] * 2,
        compiler_params=SMALL,
        name=f"last{b}",
    )(weights, up, got, *after)


def solution(mesh):
    n_tgt, n_src = mesh.shape["tgt"], mesh.shape["src"]

    def swap(v, flip_tgt, flip_src):
        return lax.ppermute(v, AXES, moves(flip_tgt, flip_src, n_tgt, n_src))

    def pieces(v, n, flip_tgt, flip_src):
        step = v.shape[0] // n
        return jnp.concatenate(
            [swap(v[i * step : (i + 1) * step], flip_tgt, flip_src) for i in range(n)]
        )

    def add(a, b):
        return a.astype(F32) + b.astype(F32)

    def pick(v, i):
        return lax.dynamic_index_in_dim(v, i, 1, False)

    def local(coefficients, factors):
        blocks, _, rows, cols = coefficients.shape
        me = lax.axis_index("src")
        x, yh = me // 4, (me // 2) % 2
        low, token = opening(factors, coefficients)
        low = [low] + list(first(factors, coefficients, range(1, blocks), True, token))
        got = [swap(v, 1, 0) for v in low]
        up, second, third = rest(factors, coefficients, low[-1])
        pairs = [None] * blocks
        order = up[0]

        def mix(b, *after):
            nonlocal order
            order, up[b] = middle(second[b], up[b], got[b], b, order, *after)
            got[b] = pieces(order, ZP, 2, 0)

        def end(b, *after):
            nonlocal order
            order, keep = last(third[b], up[b], got[b], b, order, *after)
            pairs[b] = add(keep, pieces(order, AP, 0, 1)).astype(BF).reshape(2, 4, 2, 16, cols)

        def halve(pair, near):
            back = swap(jnp.stack([pick(pair, x ^ near), pick(pair, x ^ 2)]), 0, near * 4)
            return add(jnp.stack([pick(pair, x), pick(pair, x ^ 4 - near)]), back).astype(BF)

        mix(0)
        mix(1)
        mix(2)
        end(0)
        mix(3)
        end(1)
        h0, h1 = halve(pairs[0], 1), halve(pairs[1], 3)
        end(2, pairs[0])
        end(3)
        late = jnp.stack(pairs[2:])
        shard = lambda d: lax.dynamic_index_in_dim(late, x ^ d, 2, False)
        by1 = swap(jnp.concatenate([shard(1), h1[1:]]), 0, 4)
        by3 = swap(jnp.concatenate([shard(3), h0[1:]]), 0, 12)
        by2 = swap(shard(2), 0, 8)
        sums = add(shard(0), by2) + add(by1[:2], by3[:2])
        total = jnp.stack([add(h0[0], by3[2]), add(h1[0], by1[2]), sums[0], sums[1]], axis=2)
        total = total.astype(BF)
        mine, other = pick(total, yh), pick(total, 1 - yh)
        lows = add(swap(other[1], 4, 2), swap(mine[1], 4, 0))
        ups = add(mine[0], swap(other[0], 0, 2))
        return jnp.stack([ups, lows], axis=1)

    return jax.shard_map(
        local,
        mesh=mesh,
        in_specs=(P("tgt", "src", None, None), P(None, "tgt", "src", None, None)),
        out_specs=P("tgt", None, "src", None),
        check_vma=False,
    )
```

```python
import jax
import jax.numpy as jnp
from jax import lax
from jax.experimental import pallas as pl
from jax.experimental.pallas import tpu as pltpu
from jax.sharding import PartitionSpec as P

AXES = ("tgt", "src")
BF = jnp.bfloat16
F32 = jnp.float32
VMEM = pl.BlockSpec(memory_space=pltpu.VMEM)
ANY = pl.BlockSpec(memory_space=pl.ANY)
SMALL = pltpu.CompilerParams(vmem_limit_bytes=12 << 20)
AP = 2
FLIPS = (0, 1, 3, 2)
LARGE = pltpu.CompilerParams(vmem_limit_bytes=58 << 20)


def moves(flip_tgt, flip_src, n_tgt, n_src):
    return [
        (t * n_src + s, (t ^ flip_tgt) * n_src + (s ^ flip_src))
        for t in range(n_tgt)
        for s in range(n_src)
    ]


def dot(a, b):
    return jnp.dot(a, b, preferred_element_type=F32)


def opening(factors, coefficients):
    _, _, rows, cols = coefficients.shape
    half = rows // 2

    def kernel(f_hbm, c_hbm, o_ref, token_ref, f_ref, c_ref, sems):
        copies = [
            pltpu.make_async_copy(f_hbm.at[0, 0, 0, pl.ds(half, half)], f_ref, sems.at[0]),
            pltpu.make_async_copy(c_hbm.at[0, 0], c_ref, sems.at[1]),
        ]
        for copy in copies:
            copy.start()
        for copy in copies:
            copy.wait()
        o_ref[...] = dot(f_ref[...], c_ref[...]).astype(BF)
        token_ref[...] = c_ref[:16, :128]

    return pl.pallas_call(
        kernel,
        in_specs=[ANY, ANY],
        out_specs=[VMEM, VMEM],
        out_shape=[jax.ShapeDtypeStruct((half, cols), BF), jax.ShapeDtypeStruct((16, 128), BF)],
        scratch_shapes=[
            pltpu.VMEM((half, rows), BF),
            pltpu.VMEM((rows, cols), BF),
            pltpu.SemaphoreType.DMA((2,)),
        ],
        compiler_params=LARGE,
        name="opening",
    )(factors, coefficients)


def first(factors, coefficients, blocks, below, *after):
    _, _, rows, cols = coefficients.shape
    half = rows // 2
    top = half if below else 0

    def kernel(f_ref, c_ref, *refs):
        for b, out in zip(blocks, refs[len(after) :]):
            out[...] = dot(f_ref[0, b, 0, top : top + half], c_ref[b, 0]).astype(BF)

    return pl.pallas_call(
        kernel,
        in_specs=[VMEM] * (2 + len(after)),
        out_specs=[VMEM] * len(blocks),
        out_shape=[jax.ShapeDtypeStruct((half, cols), BF)] * len(blocks),
        compiler_params=SMALL,
        name="lower" if below else "upper",
    )(factors, coefficients, *after)


def rest(factors, coefficients, after):
    blocks, _, rows, cols = coefficients.shape
    half = rows // 2

    def kernel(f_ref, c_ref, _, *refs):
        outs, later, sems = refs[:blocks], refs[blocks:-1], refs[-1]
        copies = [
            pltpu.make_async_copy(f_ref.at[1 + i // blocks, i % blocks, 0], later[i], sems.at[i])
            for i in range(2 * blocks)
        ]
        for copy in copies:
            copy.start()
        for b, out in enumerate(outs):
            out[...] = dot(f_ref[0, b, 0, :half], c_ref[b, 0]).astype(BF)
        for copy in copies:
            copy.wait()

    out = pl.pallas_call(
        kernel,
        in_specs=[VMEM] * 3,
        out_specs=[VMEM] * 3 * blocks,
        out_shape=[jax.ShapeDtypeStruct((half, cols), BF)] * blocks
        + [jax.ShapeDtypeStruct((rows, rows), BF)] * (2 * blocks),
        scratch_shapes=[pltpu.SemaphoreType.DMA((2 * blocks,))],
        compiler_params=SMALL,
        name="upper",
    )(factors, coefficients, after)
    return list(out[:blocks]), out[blocks : 2 * blocks], out[2 * blocks :]


def middle(weights, up, got, b, *after):
    half, cols = got.shape

    def kernel(f_ref, u_ref, g_ref, *refs):
        low_ref, up_ref = refs[len(after) :]
        w = f_ref
        u, g = u_ref[...], g_ref[...]
        low_ref[...] = (dot(w[half:, :half], u) + dot(w[half:, half:], g)).astype(BF)
        up_ref[...] = (dot(w[:half, :half], u) + dot(w[:half, half:], g)).astype(BF)

    return pl.pallas_call(
        kernel,
        in_specs=[VMEM] * (3 + len(after)),
        out_specs=[VMEM, VMEM],
        out_shape=[jax.ShapeDtypeStruct((half, cols), BF)] * 2,
        compiler_params=SMALL,
        name=f"middle{b}",
    )(weights, up, got, *after)


def last(weights, up, got, b, *after):
    half, cols = got.shape

    def kernel(f_ref, u_ref, g_ref, *refs):
        keep_ref, *gives = refs[len(after) :]
        step = half // len(gives)
        even = lax.rem(lax.axis_index("src"), 2) == 0
        w = f_ref
        u, g = u_ref[...], g_ref[...]
        out = (dot(w[:, :half], u) + dot(w[:, half:], g)).astype(BF)
        for i in range(2 * half // 32):
            one, two = out[i * 32 : i * 32 + 16], out[i * 32 + 16 : i * 32 + 32]
            keep_ref[i * 16 : i * 16 + 16] = jnp.where(even, one, two)
            at = i * 16 % step
            gives[i * 16 // step][at : at + 16] = jnp.where(even, two, one)

    return pl.pallas_call(
        kernel,
        in_specs=[VMEM] * (3 + len(after)),
        out_specs=[VMEM] * (1 + AP),
        out_shape=[jax.ShapeDtypeStruct((half, cols), BF)]
        + [jax.ShapeDtypeStruct((half // AP, cols), BF)] * AP,
        compiler_params=SMALL,
        name=f"last{b}",
    )(weights, up, got, *after)


def pack(keeps, backs):
    half, cols = keeps[0].shape
    n = len(keeps)
    piece = half // 8

    def kernel(*refs):
        kept, got, outs = refs[:n], refs[n : n * (1 + AP)], refs[n * (1 + AP) :]
        x = lax.axis_index("src") // 4
        for out, d in zip(outs, FLIPS):
            for b in range(n):
                for h in range(2):
                    row = h * half // 2
                    part = got[b * AP + row * AP // half]
                    at = pl.multiple_of((x ^ d) * piece, piece)
                    one = kept[b][pl.ds(row + at, piece)].astype(F32)
                    two = part[pl.ds(row % (half // AP) + at, piece)].astype(F32)
                    to = (b * 2 + h) * piece
                    out[to : to + piece] = (one + two).astype(BF)

    return pl.pallas_call(
        kernel,
        in_specs=[VMEM] * (n * (1 + AP)),
        out_specs=[VMEM] * 4,
        out_shape=[jax.ShapeDtypeStruct((n * 2 * piece, cols), BF)] * 4,
        compiler_params=SMALL,
        name="pack",
    )(*keeps, *[v for back in backs for v in back])


def split(groups):
    n = len(groups)
    cols = groups[0][0].shape[1]
    counts = [group[0].shape[0] // 64 for group in groups]

    def kernel(*refs):
        ins, outs = refs[: 4 * n], refs[4 * n :]
        yh = lax.rem(lax.axis_index("src") // 2, 2)
        first = 0
        for g, count in enumerate(counts):
            for b in range(count):
                for h in range(2):
                    for k in range(2):
                        at = (b * 2 + h) * 32 + pl.multiple_of((yh ^ k) * 16, 16)
                        parts = [ref[pl.ds(at, 16)].astype(F32) for ref in ins[4 * g : 4 * g + 4]]
                        total = (parts[0] + parts[1]) + (parts[2] + parts[3])
                        to = (first + b) * 16
                        outs[2 * h + k][to : to + 16] = total.astype(BF)
            first += count

    return pl.pallas_call(
        kernel,
        in_specs=[VMEM] * (4 * n),
        out_specs=[VMEM] * 4,
        out_shape=[jax.ShapeDtypeStruct((16 * sum(counts), cols), BF)] * 4,
        compiler_params=SMALL,
        name="split",
    )(*[v for group in groups for v in group])


def finish(up_one, up_two, low_one, low_two):
    rows, cols = up_one.shape
    blocks = rows // 16

    def kernel(*refs):
        out = refs[4]
        for h in range(2):
            one, two = refs[2 * h], refs[2 * h + 1]
            for b in range(blocks):
                rows = slice(b * 16, b * 16 + 16)
                out[b, h] = one[rows].astype(F32) + two[rows].astype(F32)

    return pl.pallas_call(
        kernel,
        in_specs=[VMEM] * 4,
        out_specs=VMEM,
        out_shape=jax.ShapeDtypeStruct((blocks, 2, 16, cols), F32),
        compiler_params=SMALL,
        name="finish",
    )(up_one, up_two, low_one, low_two)


def solution(mesh):
    n_tgt, n_src = mesh.shape["tgt"], mesh.shape["src"]

    def swap(v, flip_tgt, flip_src):
        return lax.ppermute(v, AXES, moves(flip_tgt, flip_src, n_tgt, n_src))

    def local(coefficients, factors):
        blocks = coefficients.shape[0]
        low, token = opening(factors, coefficients)
        low = [low] + list(first(factors, coefficients, range(1, blocks), True, token))
        got = [swap(v, 1, 0) for v in low]
        up, second, third = rest(factors, coefficients, low[-1])
        keeps, backs = [None] * blocks, [None] * blocks
        order = up[0]

        def mix(b, *after):
            nonlocal order
            order, up[b] = middle(second[b], up[b], got[b], b, order, *after)
            got[b] = swap(order, 2, 0)

        def end(b, *after):
            nonlocal order
            keeps[b], *gives = last(third[b], up[b], got[b], b, order, *after)
            order = gives[0]
            backs[b] = [swap(v, 0, 1) for v in gives]

        def across(*group):
            own, *gives = pack([keeps[b] for b in group], [backs[b] for b in group])
            return [own] + [swap(v, 0, d * 4) for v, d in zip(gives, FLIPS[1:])]

        mix(0)
        mix(1)
        mix(2)
        end(0)
        mix(3)
        end(1)
        early = across(0, 1)
        end(2)
        end(3, early[1], early[2], early[3])
        late = across(2, 3)
        up_mine, up_other, low_mine, low_other = split([early, late])
        return finish(up_mine, swap(up_other, 0, 2), swap(low_other, 4, 2), swap(low_mine, 4, 0))

    return jax.shard_map(
        local,
        mesh=mesh,
        in_specs=(P("tgt", "src", None, None), P(None, "tgt", "src", None, None)),
        out_specs=P("tgt", None, "src", None),
        check_vma=False,
    )
```

```python
import jax
import jax.numpy as jnp
from jax import lax
from jax.experimental import pallas as pl
from jax.experimental.pallas import tpu as pltpu
from jax.sharding import PartitionSpec as P

AXES = ("tgt", "src")
BF = jnp.bfloat16
F32 = jnp.float32
VMEM = pl.BlockSpec(memory_space=pltpu.VMEM)
ANY = pl.BlockSpec(memory_space=pl.ANY)
SMALL = pltpu.CompilerParams(vmem_limit_bytes=12 << 20)
AP = 2
FLIPS = (0, 1, 3, 2)
LARGE = pltpu.CompilerParams(vmem_limit_bytes=58 << 20)


def moves(flip_tgt, flip_src, n_tgt, n_src):
    return [
        (t * n_src + s, (t ^ flip_tgt) * n_src + (s ^ flip_src))
        for t in range(n_tgt)
        for s in range(n_src)
    ]


def dot(a, b):
    return jnp.dot(a, b, preferred_element_type=F32)


def opening(factors, coefficients):
    _, _, rows, cols = coefficients.shape
    half = rows // 2

    def kernel(f_hbm, c_hbm, o_ref, token_ref, f_ref, c_ref, sems):
        copies = [
            pltpu.make_async_copy(f_hbm.at[0, 0, 0, pl.ds(half, half)], f_ref, sems.at[0]),
            pltpu.make_async_copy(c_hbm.at[0, 0], c_ref, sems.at[1]),
        ]
        for copy in copies:
            copy.start()
        for copy in copies:
            copy.wait()
        o_ref[...] = dot(f_ref[...], c_ref[...]).astype(BF)
        token_ref[...] = c_ref[:16, :128]

    return pl.pallas_call(
        kernel,
        in_specs=[ANY, ANY],
        out_specs=[VMEM, VMEM],
        out_shape=[jax.ShapeDtypeStruct((half, cols), BF), jax.ShapeDtypeStruct((16, 128), BF)],
        scratch_shapes=[
            pltpu.VMEM((half, rows), BF),
            pltpu.VMEM((rows, cols), BF),
            pltpu.SemaphoreType.DMA((2,)),
        ],
        compiler_params=LARGE,
        name="opening",
    )(factors, coefficients)


def first(factors, coefficients, blocks, below, *after):
    _, _, rows, cols = coefficients.shape
    half = rows // 2
    top = half if below else 0

    def kernel(f_ref, c_ref, *refs):
        for b, out in zip(blocks, refs[len(after) :]):
            out[...] = dot(f_ref[0, b, 0, top : top + half], c_ref[b, 0]).astype(BF)

    return pl.pallas_call(
        kernel,
        in_specs=[VMEM] * (2 + len(after)),
        out_specs=[VMEM] * len(blocks),
        out_shape=[jax.ShapeDtypeStruct((half, cols), BF)] * len(blocks),
        compiler_params=SMALL,
        name="lower" if below else "upper",
    )(factors, coefficients, *after)


def rest(factors, coefficients, after):
    blocks, _, rows, cols = coefficients.shape
    half = rows // 2

    def kernel(f_ref, c_ref, _, *refs):
        outs, later, sems = refs[:blocks], refs[blocks:-1], refs[-1]
        copies = [
            pltpu.make_async_copy(f_ref.at[1 + i // blocks, i % blocks, 0], later[i], sems.at[i])
            for i in range(2 * blocks)
        ]
        for copy in copies:
            copy.start()
        for b, out in enumerate(outs):
            out[...] = dot(f_ref[0, b, 0, :half], c_ref[b, 0]).astype(BF)
        for copy in copies:
            copy.wait()

    out = pl.pallas_call(
        kernel,
        in_specs=[VMEM] * 3,
        out_specs=[VMEM] * 3 * blocks,
        out_shape=[jax.ShapeDtypeStruct((half, cols), BF)] * blocks
        + [jax.ShapeDtypeStruct((rows, rows), BF)] * (2 * blocks),
        scratch_shapes=[pltpu.SemaphoreType.DMA((2 * blocks,))],
        compiler_params=SMALL,
        name="upper",
    )(factors, coefficients, after)
    return list(out[:blocks]), out[blocks : 2 * blocks], out[2 * blocks :]


def middle(weights, up, got, b, *after):
    half, cols = got.shape

    def kernel(f_ref, u_ref, g_ref, *refs):
        low_ref, up_ref = refs[len(after) :]
        w = f_ref
        u, g = u_ref[...], g_ref[...]
        low_ref[...] = (dot(w[half:, :half], u) + dot(w[half:, half:], g)).astype(BF)
        up_ref[...] = (dot(w[:half, :half], u) + dot(w[:half, half:], g)).astype(BF)

    return pl.pallas_call(
        kernel,
        in_specs=[VMEM] * (3 + len(after)),
        out_specs=[VMEM, VMEM],
        out_shape=[jax.ShapeDtypeStruct((half, cols), BF)] * 2,
        compiler_params=SMALL,
        name=f"middle{b}",
    )(weights, up, got, *after)


def last(weights, up, got, b, *after):
    half, cols = got.shape

    def kernel(f_ref, u_ref, g_ref, *refs):
        keep_ref, *gives = refs[len(after) :]
        step = half // len(gives)
        even = lax.rem(lax.axis_index("src"), 2) == 0
        w = f_ref
        u, g = u_ref[...], g_ref[...]
        out = (dot(w[:, :half], u) + dot(w[:, half:], g)).astype(BF)
        for i in range(2 * half // 32):
            one, two = out[i * 32 : i * 32 + 16], out[i * 32 + 16 : i * 32 + 32]
            keep_ref[i * 16 : i * 16 + 16] = jnp.where(even, one, two)
            at = i * 16 % step
            gives[i * 16 // step][at : at + 16] = jnp.where(even, two, one)

    return pl.pallas_call(
        kernel,
        in_specs=[VMEM] * (3 + len(after)),
        out_specs=[VMEM] * (1 + AP),
        out_shape=[jax.ShapeDtypeStruct((half, cols), BF)]
        + [jax.ShapeDtypeStruct((half // AP, cols), BF)] * AP,
        compiler_params=SMALL,
        name=f"last{b}",
    )(weights, up, got, *after)


def pack(keeps, backs):
    half, cols = keeps[0].shape
    n = len(keeps)
    piece = half // 8

    def kernel(*refs):
        kept, got, outs = refs[:n], refs[n : n * (1 + AP)], refs[n * (1 + AP) :]
        x = lax.axis_index("src") // 4
        for out, d in zip(outs, FLIPS):
            for b in range(n):
                for h in range(2):
                    row = h * half // 2
                    part = got[b * AP + row * AP // half]
                    at = pl.multiple_of((x ^ d) * piece, piece)
                    one = kept[b][pl.ds(row + at, piece)].astype(F32)
                    two = part[pl.ds(row % (half // AP) + at, piece)].astype(F32)
                    to = (b * 2 + h) * piece
                    out[to : to + piece] = (one + two).astype(BF)

    return pl.pallas_call(
        kernel,
        in_specs=[VMEM] * (n * (1 + AP)),
        out_specs=[VMEM] * 4,
        out_shape=[jax.ShapeDtypeStruct((n * 2 * piece, cols), BF)] * 4,
        compiler_params=SMALL,
        name="pack",
    )(*keeps, *[v for back in backs for v in back])


def split(groups):
    n = len(groups)
    cols = groups[0][0].shape[1]
    counts = [group[0].shape[0] // 64 for group in groups]

    def kernel(*refs):
        ins, outs = refs[: 4 * n], refs[4 * n :]
        yh = lax.rem(lax.axis_index("src") // 2, 2)
        first = 0
        for g, count in enumerate(counts):
            for b in range(count):
                for h in range(2):
                    for k in range(2):
                        at = (b * 2 + h) * 32 + pl.multiple_of((yh ^ k) * 16, 16)
                        parts = [ref[pl.ds(at, 16)].astype(F32) for ref in ins[4 * g : 4 * g + 4]]
                        total = (parts[0] + parts[1]) + (parts[2] + parts[3])
                        to = (first + b) * 16
                        outs[2 * h + k][to : to + 16] = total.astype(BF)
            first += count

    return pl.pallas_call(
        kernel,
        in_specs=[VMEM] * (4 * n),
        out_specs=[VMEM] * 4,
        out_shape=[jax.ShapeDtypeStruct((16 * sum(counts), cols), BF)] * 4,
        compiler_params=SMALL,
        name="split",
    )(*[v for group in groups for v in group])


def lows(one, two):
    def kernel(one_ref, two_ref, out_ref):
        out_ref[...] = one_ref[...].astype(F32) + two_ref[...].astype(F32)

    return pl.pallas_call(
        kernel,
        in_specs=[VMEM] * 2,
        out_specs=VMEM,
        out_shape=jax.ShapeDtypeStruct(one.shape, F32),
        compiler_params=SMALL,
        name="lows",
    )(one, two)


def finish(up_one, up_two, low):
    rows, cols = low.shape
    blocks = rows // 16

    def kernel(one_ref, two_ref, low_ref, out_ref):
        for b in range(blocks):
            at = slice(b * 16, b * 16 + 16)
            out_ref[b, 0] = one_ref[at].astype(F32) + two_ref[at].astype(F32)
            out_ref[b, 1] = low_ref[at]

    return pl.pallas_call(
        kernel,
        in_specs=[VMEM] * 3,
        out_specs=VMEM,
        out_shape=jax.ShapeDtypeStruct((blocks, 2, 16, cols), F32),
        compiler_params=SMALL,
        name="finish",
    )(up_one, up_two, low)


def solution(mesh):
    n_tgt, n_src = mesh.shape["tgt"], mesh.shape["src"]

    def swap(v, flip_tgt, flip_src):
        return lax.ppermute(v, AXES, moves(flip_tgt, flip_src, n_tgt, n_src))

    def local(coefficients, factors):
        blocks = coefficients.shape[0]
        low, token = opening(factors, coefficients)
        low = [low] + list(first(factors, coefficients, range(1, blocks), True, token))
        got = [swap(v, 1, 0) for v in low]
        up, second, third = rest(factors, coefficients, low[-1])
        keeps, backs = [None] * blocks, [None] * blocks
        order = up[0]

        def mix(b, *after):
            nonlocal order
            order, up[b] = middle(second[b], up[b], got[b], b, order, *after)
            got[b] = swap(order, 2, 0)

        def end(b, *after):
            nonlocal order
            keeps[b], *gives = last(third[b], up[b], got[b], b, order, *after)
            order = gives[0]
            backs[b] = [swap(v, 0, 1) for v in gives]

        def across(*group):
            own, *gives = pack([keeps[b] for b in group], [backs[b] for b in group])
            return [own] + [swap(v, 0, d * 4) for v, d in zip(gives, FLIPS[1:])]

        mix(0)
        mix(1)
        mix(2)
        end(0)
        mix(3)
        end(1)
        early = across(0, 1)
        end(2)
        end(3, early[1], early[2], early[3])
        late = across(2, 3)
        up_mine, up_other, low_mine, low_other = split([early, late])
        low = lows(swap(low_other, 4, 2), swap(low_mine, 4, 0))
        return finish(up_mine, swap(up_other, 0, 2), low)

    return jax.shard_map(
        local,
        mesh=mesh,
        in_specs=(P("tgt", "src", None, None), P(None, "tgt", "src", None, None)),
        out_specs=P("tgt", None, "src", None),
        check_vma=False,
    )
```

```python
import jax
import jax.numpy as jnp
from jax import lax
from jax.experimental import pallas as pl
from jax.experimental.pallas import tpu as pltpu
from jax.sharding import PartitionSpec as P

AXES = ("tgt", "src")
BF = jnp.bfloat16
F32 = jnp.float32
VMEM = pl.BlockSpec(memory_space=pltpu.VMEM)
ANY = pl.BlockSpec(memory_space=pl.ANY)
SMALL = pltpu.CompilerParams(vmem_limit_bytes=12 << 20)
AP = 2
FLIPS = (0, 1, 3, 2)
LARGE = pltpu.CompilerParams(vmem_limit_bytes=58 << 20)


def moves(flip_tgt, flip_src, n_tgt, n_src):
    return [
        (t * n_src + s, (t ^ flip_tgt) * n_src + (s ^ flip_src))
        for t in range(n_tgt)
        for s in range(n_src)
    ]


def dot(a, b):
    return jnp.dot(a, b, preferred_element_type=F32)


def opening(factors, coefficients):
    _, _, rows, cols = coefficients.shape
    half = rows // 2

    def kernel(f_hbm, c_hbm, o_ref, token_ref, f_ref, c_ref, sems):
        copies = [
            pltpu.make_async_copy(f_hbm.at[0, 0, 0, pl.ds(half, half)], f_ref, sems.at[0]),
            pltpu.make_async_copy(c_hbm.at[0, 0], c_ref, sems.at[1]),
        ]
        for copy in copies:
            copy.start()
        for copy in copies:
            copy.wait()
        o_ref[...] = dot(f_ref[...], c_ref[...]).astype(BF)
        token_ref[...] = c_ref[:16, :128]

    return pl.pallas_call(
        kernel,
        in_specs=[ANY, ANY],
        out_specs=[VMEM, VMEM],
        out_shape=[jax.ShapeDtypeStruct((half, cols), BF), jax.ShapeDtypeStruct((16, 128), BF)],
        scratch_shapes=[
            pltpu.VMEM((half, rows), BF),
            pltpu.VMEM((rows, cols), BF),
            pltpu.SemaphoreType.DMA((2,)),
        ],
        compiler_params=LARGE,
        name="opening",
    )(factors, coefficients)


def first(factors, coefficients, blocks, below, *after):
    _, _, rows, cols = coefficients.shape
    half = rows // 2
    top = half if below else 0

    def kernel(f_ref, c_ref, *refs):
        for b, out in zip(blocks, refs[len(after) :]):
            out[...] = dot(f_ref[0, b, 0, top : top + half], c_ref[b, 0]).astype(BF)

    return pl.pallas_call(
        kernel,
        in_specs=[VMEM] * (2 + len(after)),
        out_specs=[VMEM] * len(blocks),
        out_shape=[jax.ShapeDtypeStruct((half, cols), BF)] * len(blocks),
        compiler_params=SMALL,
        name="lower" if below else "upper",
    )(factors, coefficients, *after)


def rest(factors, coefficients, after):
    blocks, _, rows, cols = coefficients.shape
    half = rows // 2

    def kernel(f_ref, c_ref, _, *refs):
        outs, later, sems = refs[:blocks], refs[blocks:-1], refs[-1]
        copies = [
            pltpu.make_async_copy(f_ref.at[1 + i // blocks, i % blocks, 0], later[i], sems.at[i])
            for i in range(2 * blocks)
        ]
        for copy in copies:
            copy.start()
        for b, out in enumerate(outs):
            out[...] = dot(f_ref[0, b, 0, :half], c_ref[b, 0]).astype(BF)
        for copy in copies:
            copy.wait()

    out = pl.pallas_call(
        kernel,
        in_specs=[VMEM] * 3,
        out_specs=[VMEM] * 3 * blocks,
        out_shape=[jax.ShapeDtypeStruct((half, cols), BF)] * blocks
        + [jax.ShapeDtypeStruct((rows, rows), BF)] * (2 * blocks),
        scratch_shapes=[pltpu.SemaphoreType.DMA((2 * blocks,))],
        compiler_params=SMALL,
        name="upper",
    )(factors, coefficients, after)
    return list(out[:blocks]), out[blocks : 2 * blocks], out[2 * blocks :]


def middle(weights, up, got, b, *after):
    half, cols = got.shape

    def kernel(f_ref, u_ref, g_ref, *refs):
        low_ref, up_ref = refs[len(after) :]
        w = f_ref
        u, g = u_ref[...], g_ref[...]
        low_ref[...] = (dot(w[half:, :half], u) + dot(w[half:, half:], g)).astype(BF)
        up_ref[...] = (dot(w[:half, :half], u) + dot(w[:half, half:], g)).astype(BF)

    return pl.pallas_call(
        kernel,
        in_specs=[VMEM] * (3 + len(after)),
        out_specs=[VMEM, VMEM],
        out_shape=[jax.ShapeDtypeStruct((half, cols), BF)] * 2,
        compiler_params=SMALL,
        name=f"middle{b}",
    )(weights, up, got, *after)


def last(weights, up, got, b, *after):
    half, cols = got.shape

    def kernel(f_ref, u_ref, g_ref, *refs):
        keep_ref, *gives = refs[len(after) :]
        step = half // len(gives)
        even = lax.rem(lax.axis_index("src"), 2) == 0
        w = f_ref
        u, g = u_ref[...], g_ref[...]
        out = (dot(w[:, :half], u) + dot(w[:, half:], g)).astype(BF)
        for i in range(2 * half // 32):
            one, two = out[i * 32 : i * 32 + 16], out[i * 32 + 16 : i * 32 + 32]
            keep_ref[i * 16 : i * 16 + 16] = jnp.where(even, one, two)
            at = i * 16 % step
            gives[i * 16 // step][at : at + 16] = jnp.where(even, two, one)

    return pl.pallas_call(
        kernel,
        in_specs=[VMEM] * (3 + len(after)),
        out_specs=[VMEM] * (1 + AP),
        out_shape=[jax.ShapeDtypeStruct((half, cols), BF)]
        + [jax.ShapeDtypeStruct((half // AP, cols), BF)] * AP,
        compiler_params=SMALL,
        name=f"last{b}",
    )(weights, up, got, *after)


def pack(keeps, backs):
    half, cols = keeps[0].shape
    n = len(keeps)
    piece = half // 8

    def kernel(*refs):
        kept, got, outs = refs[:n], refs[n : n * (1 + AP)], refs[n * (1 + AP) :]
        x = lax.axis_index("src") // 4
        for out, d in zip(outs, FLIPS):
            for b in range(n):
                for h in range(2):
                    row = h * half // 2
                    part = got[b * AP + row * AP // half]
                    at = pl.multiple_of((x ^ d) * piece, piece)
                    one = kept[b][pl.ds(row + at, piece)].astype(F32)
                    two = part[pl.ds(row % (half // AP) + at, piece)].astype(F32)
                    to = (b * 2 + h) * piece
                    out[to : to + piece] = (one + two).astype(BF)

    return pl.pallas_call(
        kernel,
        in_specs=[VMEM] * (n * (1 + AP)),
        out_specs=[VMEM] * 4,
        out_shape=[jax.ShapeDtypeStruct((n * 2 * piece, cols), BF)] * 4,
        compiler_params=SMALL,
        name="pack",
    )(*keeps, *[v for back in backs for v in back])


def shares(parts, outs, k):
    yh = lax.rem(lax.axis_index("src") // 2, 2)
    for b in range(parts[0].shape[0] // 64):
        for h, out in enumerate(outs):
            at = (b * 2 + h) * 32 + pl.multiple_of((yh ^ k) * 16, 16)
            one, two, three, four = [ref[pl.ds(at, 16)].astype(F32) for ref in parts]
            out[b * 16 : b * 16 + 16] = ((one + two) + (three + four)).astype(BF)


def split(parts):
    rows, cols = parts[0].shape
    rows //= 4

    def kernel(*refs):
        up_ref, low_ref, other_ref = refs[4:]
        shares(refs[:4], (up_ref, low_ref), 0)
        shares(refs[:4], (other_ref.at[:rows], other_ref.at[rows:]), 1)

    return pl.pallas_call(
        kernel,
        in_specs=[VMEM] * 4,
        out_specs=[VMEM] * 3,
        out_shape=[jax.ShapeDtypeStruct((n, cols), BF) for n in (rows, rows, 2 * rows)],
        compiler_params=SMALL,
        name="split",
    )(*parts)


def gather(parts, low, got):
    rows, cols = parts[0].shape
    rows //= 4

    def kernel(*refs):
        low_ref, got_ref, up_ref, up_other_ref, low_other_ref, send_ref = refs[4:]
        shares(refs[:4], (up_other_ref, low_other_ref), 1)
        shares(refs[:4], (up_ref, send_ref.at[:rows]), 0)
        both = low_ref[...].astype(F32) + got_ref[rows:].astype(F32)
        send_ref[rows:] = both.astype(BF)

    return pl.pallas_call(
        kernel,
        in_specs=[VMEM] * 6,
        out_specs=[VMEM] * 4,
        out_shape=[jax.ShapeDtypeStruct((n, cols), BF) for n in (rows, rows, rows, 2 * rows)],
        compiler_params=SMALL,
        name="gather",
    )(*parts, low, got)


def lows(one, two):
    rows, cols = one.shape

    def kernel(one_ref, two_ref, out_ref):
        out_ref[:rows] = two_ref[rows:].astype(F32)
        out_ref[rows:] = one_ref[...].astype(F32) + two_ref[:rows].astype(F32)

    return pl.pallas_call(
        kernel,
        in_specs=[VMEM] * 2,
        out_specs=VMEM,
        out_shape=jax.ShapeDtypeStruct((2 * rows, cols), F32),
        compiler_params=SMALL,
        name="lows",
    )(one, two)


def finish(early, late, low):
    rows, cols = low.shape
    blocks = rows // 16

    def kernel(*refs):
        ups, low_ref, out_ref = refs[:4], refs[4], refs[5]
        for b in range(blocks):
            one, two = ups[:2] if b < blocks // 2 else ups[2:]
            at = slice(b % (blocks // 2) * 16, b % (blocks // 2) * 16 + 16)
            out_ref[b, 0] = one[at].astype(F32) + two[at].astype(F32)
            out_ref[b, 1] = low_ref[b * 16 : b * 16 + 16]

    return pl.pallas_call(
        kernel,
        in_specs=[VMEM] * 5,
        out_specs=VMEM,
        out_shape=jax.ShapeDtypeStruct((blocks, 2, 16, cols), F32),
        compiler_params=SMALL,
        name="finish",
    )(*early, *late, low)


def solution(mesh):
    n_tgt, n_src = mesh.shape["tgt"], mesh.shape["src"]

    def swap(v, flip_tgt, flip_src):
        return lax.ppermute(v, AXES, moves(flip_tgt, flip_src, n_tgt, n_src))

    def local(coefficients, factors):
        blocks = coefficients.shape[0]
        low, token = opening(factors, coefficients)
        low = [low] + list(first(factors, coefficients, range(1, blocks), True, token))
        got = [swap(v, 1, 0) for v in low]
        up, second, third = rest(factors, coefficients, low[-1])
        keeps, backs = [None] * blocks, [None] * blocks
        order = up[0]

        def mix(b, *after):
            nonlocal order
            order, up[b] = middle(second[b], up[b], got[b], b, order, *after)
            got[b] = swap(order, 2, 0)

        def end(b, *after):
            nonlocal order
            keeps[b], *gives = last(third[b], up[b], got[b], b, order, *after)
            order = gives[0]
            backs[b] = [swap(v, 0, 1) for v in gives]

        def across(*group):
            own, *gives = pack([keeps[b] for b in group], [backs[b] for b in group])
            return [own] + [swap(v, 0, d * 4) for v, d in zip(gives, FLIPS[1:])]

        mix(0)
        mix(1)
        mix(2)
        end(0)
        mix(3)
        end(1)
        early = across(0, 1)
        end(2)
        end(3, early[1], early[2], early[3])
        late = across(2, 3)
        up, low, other = split(early)
        got = swap(other, 0, 2)
        late_up, up_other, low_other, send = gather(late, low, got)
        low = lows(swap(low_other, 4, 2), swap(send, 4, 0))
        return finish((up, got), (late_up, swap(up_other, 0, 2)), low)

    return jax.shard_map(
        local,
        mesh=mesh,
        in_specs=(P("tgt", "src", None, None), P(None, "tgt", "src", None, None)),
        out_specs=P("tgt", None, "src", None),
        check_vma=False,
    )
```

```python
import jax
import jax.numpy as jnp
from jax import lax
from jax.experimental import pallas as pl
from jax.experimental.pallas import tpu as pltpu
from jax.sharding import PartitionSpec as P

AXES = ("tgt", "src")
BF = jnp.bfloat16
F32 = jnp.float32
VMEM = pl.BlockSpec(memory_space=pltpu.VMEM)
ANY = pl.BlockSpec(memory_space=pl.ANY)
SMALL = pltpu.CompilerParams(vmem_limit_bytes=12 << 20)
AP = 2
FLIPS = (0, 1, 3, 2)
LARGE = pltpu.CompilerParams(vmem_limit_bytes=58 << 20)


def moves(flip_tgt, flip_src, n_tgt, n_src):
    return [
        (t * n_src + s, (t ^ flip_tgt) * n_src + (s ^ flip_src))
        for t in range(n_tgt)
        for s in range(n_src)
    ]


def dot(a, b):
    return jnp.dot(a, b, preferred_element_type=F32)


def opening(factors, coefficients):
    _, _, rows, cols = coefficients.shape
    half = rows // 2

    def kernel(f_hbm, c_hbm, o_ref, token_ref, f_ref, c_ref, sems):
        copies = [
            pltpu.make_async_copy(f_hbm.at[0, 0, 0, pl.ds(half, half)], f_ref, sems.at[0]),
            pltpu.make_async_copy(c_hbm.at[0, 0], c_ref, sems.at[1]),
        ]
        for copy in copies:
            copy.start()
        for copy in copies:
            copy.wait()
        o_ref[...] = dot(f_ref[...], c_ref[...]).astype(BF)
        token_ref[...] = c_ref[:16, :128]

    return pl.pallas_call(
        kernel,
        in_specs=[ANY, ANY],
        out_specs=[VMEM, VMEM],
        out_shape=[jax.ShapeDtypeStruct((half, cols), BF), jax.ShapeDtypeStruct((16, 128), BF)],
        scratch_shapes=[
            pltpu.VMEM((half, rows), BF),
            pltpu.VMEM((rows, cols), BF),
            pltpu.SemaphoreType.DMA((2,)),
        ],
        compiler_params=LARGE,
        name="opening",
    )(factors, coefficients)


def first(factors, coefficients, blocks, below, *after):
    _, _, rows, cols = coefficients.shape
    half = rows // 2
    top = half if below else 0

    def kernel(f_ref, c_ref, *refs):
        for b, out in zip(blocks, refs[len(after) :]):
            out[...] = dot(f_ref[0, b, 0, top : top + half], c_ref[b, 0]).astype(BF)

    return pl.pallas_call(
        kernel,
        in_specs=[VMEM] * (2 + len(after)),
        out_specs=[VMEM] * len(blocks),
        out_shape=[jax.ShapeDtypeStruct((half, cols), BF)] * len(blocks),
        compiler_params=SMALL,
        name="lower" if below else "upper",
    )(factors, coefficients, *after)


def rest(factors, coefficients, after):
    blocks, _, rows, cols = coefficients.shape
    half = rows // 2

    def kernel(f_ref, c_ref, _, *refs):
        outs, later, sems = refs[:blocks], refs[blocks:-1], refs[-1]
        copies = [
            pltpu.make_async_copy(f_ref.at[1 + i // blocks, i % blocks, 0], later[i], sems.at[i])
            for i in range(2 * blocks)
        ]
        for copy in copies:
            copy.start()
        for b, out in enumerate(outs):
            out[...] = dot(f_ref[0, b, 0, :half], c_ref[b, 0]).astype(BF)
        for copy in copies:
            copy.wait()

    out = pl.pallas_call(
        kernel,
        in_specs=[VMEM] * 3,
        out_specs=[VMEM] * 3 * blocks,
        out_shape=[jax.ShapeDtypeStruct((half, cols), BF)] * blocks
        + [jax.ShapeDtypeStruct((rows, rows), BF)] * (2 * blocks),
        scratch_shapes=[pltpu.SemaphoreType.DMA((2 * blocks,))],
        compiler_params=SMALL,
        name="upper",
    )(factors, coefficients, after)
    return list(out[:blocks]), out[blocks : 2 * blocks], out[2 * blocks :]


def middle(weights, up, got, b, *after):
    half, cols = got.shape

    def kernel(f_ref, u_ref, g_ref, *refs):
        low_ref, up_ref = refs[len(after) :]
        w = f_ref
        u, g = u_ref[...], g_ref[...]
        low_ref[...] = (dot(w[half:, :half], u) + dot(w[half:, half:], g)).astype(BF)
        up_ref[...] = (dot(w[:half, :half], u) + dot(w[:half, half:], g)).astype(BF)

    return pl.pallas_call(
        kernel,
        in_specs=[VMEM] * (3 + len(after)),
        out_specs=[VMEM, VMEM],
        out_shape=[jax.ShapeDtypeStruct((half, cols), BF)] * 2,
        compiler_params=SMALL,
        name=f"middle{b}",
    )(weights, up, got, *after)


def last(weights, up, got, b, *after):
    half, cols = got.shape

    def kernel(f_ref, u_ref, g_ref, *refs):
        keep_ref, *gives = refs[len(after) :]
        step = half // len(gives)
        even = lax.rem(lax.axis_index("src"), 2) == 0
        w = f_ref
        u, g = u_ref[...], g_ref[...]
        out = (dot(w[:, :half], u) + dot(w[:, half:], g)).astype(BF)
        for i in range(2 * half // 32):
            one, two = out[i * 32 : i * 32 + 16], out[i * 32 + 16 : i * 32 + 32]
            keep_ref[i * 16 : i * 16 + 16] = jnp.where(even, one, two)
            at = i * 16 % step
            gives[i * 16 // step][at : at + 16] = jnp.where(even, two, one)

    return pl.pallas_call(
        kernel,
        in_specs=[VMEM] * (3 + len(after)),
        out_specs=[VMEM] * (1 + AP),
        out_shape=[jax.ShapeDtypeStruct((half, cols), BF)]
        + [jax.ShapeDtypeStruct((half // AP, cols), BF)] * AP,
        compiler_params=SMALL,
        name=f"last{b}",
    )(weights, up, got, *after)


def pack(keeps, backs):
    half, cols = keeps[0].shape
    n = len(keeps)
    piece = half // 8

    def kernel(*refs):
        kept, got, outs = refs[:n], refs[n : n * (1 + AP)], refs[n * (1 + AP) :]
        x = lax.axis_index("src") // 4
        for out, d in zip(outs, FLIPS):
            for b in range(n):
                for h in range(2):
                    row = h * half // 2
                    part = got[b * AP + row * AP // half]
                    at = pl.multiple_of((x ^ d) * piece, piece)
                    one = kept[b][pl.ds(row + at, piece)].astype(F32)
                    two = part[pl.ds(row % (half // AP) + at, piece)].astype(F32)
                    to = (b * 2 + h) * piece
                    out[to : to + piece] = (one + two).astype(BF)

    return pl.pallas_call(
        kernel,
        in_specs=[VMEM] * (n * (1 + AP)),
        out_specs=[VMEM] * 4,
        out_shape=[jax.ShapeDtypeStruct((n * 2 * piece, cols), BF)] * 4,
        compiler_params=SMALL,
        name="pack",
    )(*keeps, *[v for back in backs for v in back])


def shares(parts, outs, k):
    yh = lax.rem(lax.axis_index("src") // 2, 2)
    for b in range(parts[0].shape[0] // 64):
        for h, out in enumerate(outs):
            at = (b * 2 + h) * 32 + pl.multiple_of((yh ^ k) * 16, 16)
            one, two, three, four = [ref[pl.ds(at, 16)].astype(F32) for ref in parts]
            out[b * 16 : b * 16 + 16] = ((one + two) + (three + four)).astype(BF)


def split(parts):
    rows, cols = parts[0].shape
    rows //= 4

    def kernel(*refs):
        up_ref, low_ref, other_ref = refs[4:]
        shares(refs[:4], (up_ref, low_ref), 0)
        shares(refs[:4], (other_ref.at[:rows], other_ref.at[rows:]), 1)

    return pl.pallas_call(
        kernel,
        in_specs=[VMEM] * 4,
        out_specs=[VMEM] * 3,
        out_shape=[jax.ShapeDtypeStruct((n, cols), BF) for n in (rows, rows, 2 * rows)],
        compiler_params=SMALL,
        name="split",
    )(*parts)


def gather(parts, low, got):
    rows, cols = parts[0].shape
    rows //= 4

    def kernel(*refs):
        low_ref, got_ref, up_ref, up_other_ref, low_other_ref, send_ref = refs[4:]
        shares(refs[:4], (up_other_ref, low_other_ref), 1)
        shares(refs[:4], (up_ref, send_ref.at[:rows]), 0)
        both = low_ref[...].astype(F32) + got_ref[rows:].astype(F32)
        send_ref[rows:] = both.astype(BF)

    return pl.pallas_call(
        kernel,
        in_specs=[VMEM] * 6,
        out_specs=[VMEM] * 4,
        out_shape=[jax.ShapeDtypeStruct((n, cols), BF) for n in (rows, rows, rows, 2 * rows)],
        compiler_params=SMALL,
        name="gather",
    )(*parts, low, got)


def lows(one, two):
    rows, cols = one.shape

    def kernel(one_ref, two_ref, out_ref):
        out_ref[:rows] = two_ref[rows:].astype(F32)
        out_ref[rows:] = one_ref[...].astype(F32) + two_ref[:rows].astype(F32)

    return pl.pallas_call(
        kernel,
        in_specs=[VMEM] * 2,
        out_specs=VMEM,
        out_shape=jax.ShapeDtypeStruct((2 * rows, cols), F32),
        compiler_params=SMALL,
        name="lows",
    )(one, two)


def finish(early, late, low):
    rows, cols = low.shape
    blocks = rows // 16

    def kernel(*refs):
        ups, low_ref, out_ref = refs[:4], refs[4], refs[5]
        for b in range(blocks):
            one, two = ups[:2] if b < blocks // 2 else ups[2:]
            at = slice(b % (blocks // 2) * 16, b % (blocks // 2) * 16 + 16)
            out_ref[b, 0] = one[at].astype(F32) + two[at].astype(F32)
            out_ref[b, 1] = low_ref[b * 16 : b * 16 + 16]

    return pl.pallas_call(
        kernel,
        in_specs=[VMEM] * 5,
        out_specs=VMEM,
        out_shape=jax.ShapeDtypeStruct((blocks, 2, 16, cols), F32),
        compiler_params=SMALL,
        name="finish",
    )(*early, *late, low)


def solution(mesh):
    n_tgt, n_src = mesh.shape["tgt"], mesh.shape["src"]

    def swap(v, flip_tgt, flip_src):
        return lax.ppermute(v, AXES, moves(flip_tgt, flip_src, n_tgt, n_src))

    def local(coefficients, factors):
        blocks = coefficients.shape[0]
        low, token = opening(factors, coefficients)
        low = [low] + list(first(factors, coefficients, range(1, blocks), True, token))
        got = [swap(v, 1, 0) for v in low]
        up, second, third = rest(factors, coefficients, low[-1])
        keeps, backs = [None] * blocks, [None] * blocks
        order = up[0]

        def mix(b, *after):
            nonlocal order
            order, up[b] = middle(second[b], up[b], got[b], b, order, *after)
            got[b] = swap(order, 2, 0)

        def end(b, *after):
            nonlocal order
            keeps[b], *gives = last(third[b], up[b], got[b], b, order, *after)
            order = gives[0]
            backs[b] = [swap(v, 0, 1) for v in gives]

        def across(*group):
            own, *gives = pack([keeps[b] for b in group], [backs[b] for b in group])
            return [own] + [swap(v, 0, d * 4) for v, d in zip(gives, FLIPS[1:])]

        mix(0)
        mix(1)
        mix(2)
        end(0)
        mix(3)
        end(1)
        early = across(0, 1)
        end(2)
        end(3, early[1], early[3])
        late = across(2, 3)
        up, low, other = split(early)
        got = swap(other, 0, 2)
        late_up, up_other, low_other, send = gather(late, low, got)
        low = lows(swap(low_other, 4, 2), swap(send, 4, 0))
        return finish((up, got), (late_up, swap(up_other, 0, 2)), low)

    return jax.shard_map(
        local,
        mesh=mesh,
        in_specs=(P("tgt", "src", None, None), P(None, "tgt", "src", None, None)),
        out_specs=P("tgt", None, "src", None),
        check_vma=False,
    )
```

```python
import jax
import jax.numpy as jnp
from jax import lax
from jax.experimental import pallas as pl
from jax.experimental.pallas import tpu as pltpu
from jax.sharding import PartitionSpec as P

AXES = ("tgt", "src")
BF = jnp.bfloat16
F32 = jnp.float32
VMEM = pl.BlockSpec(memory_space=pltpu.VMEM)
ANY = pl.BlockSpec(memory_space=pl.ANY)
SMALL = pltpu.CompilerParams(vmem_limit_bytes=12 << 20)
AP = 2
FLIPS = (0, 2, 1, 3)
LARGE = pltpu.CompilerParams(vmem_limit_bytes=58 << 20)


def moves(flip_tgt, flip_src, n_tgt, n_src):
    return [
        (t * n_src + s, (t ^ flip_tgt) * n_src + (s ^ flip_src))
        for t in range(n_tgt)
        for s in range(n_src)
    ]


def dot(a, b):
    return jnp.dot(a, b, preferred_element_type=F32)


def opening(factors, coefficients):
    _, _, rows, cols = coefficients.shape
    half = rows // 2

    def kernel(f_hbm, c_hbm, o_ref, token_ref, f_ref, c_ref, sems):
        copies = [
            pltpu.make_async_copy(f_hbm.at[0, 0, 0, pl.ds(half, half)], f_ref, sems.at[0]),
            pltpu.make_async_copy(c_hbm.at[0, 0], c_ref, sems.at[1]),
        ]
        for copy in copies:
            copy.start()
        for copy in copies:
            copy.wait()
        o_ref[...] = dot(f_ref[...], c_ref[...]).astype(BF)
        token_ref[...] = c_ref[:16, :128]

    return pl.pallas_call(
        kernel,
        in_specs=[ANY, ANY],
        out_specs=[VMEM, VMEM],
        out_shape=[jax.ShapeDtypeStruct((half, cols), BF), jax.ShapeDtypeStruct((16, 128), BF)],
        scratch_shapes=[
            pltpu.VMEM((half, rows), BF),
            pltpu.VMEM((rows, cols), BF),
            pltpu.SemaphoreType.DMA((2,)),
        ],
        compiler_params=LARGE,
        name="opening",
    )(factors, coefficients)


def first(factors, coefficients, blocks, below, *after):
    _, _, rows, cols = coefficients.shape
    half = rows // 2
    top = half if below else 0

    def kernel(f_ref, c_ref, *refs):
        for b, out in zip(blocks, refs[len(after) :]):
            out[...] = dot(f_ref[0, b, 0, top : top + half], c_ref[b, 0]).astype(BF)

    return pl.pallas_call(
        kernel,
        in_specs=[VMEM] * (2 + len(after)),
        out_specs=[VMEM] * len(blocks),
        out_shape=[jax.ShapeDtypeStruct((half, cols), BF)] * len(blocks),
        compiler_params=SMALL,
        name="lower" if below else "upper",
    )(factors, coefficients, *after)


def rest(factors, coefficients, after):
    blocks, _, rows, cols = coefficients.shape
    half = rows // 2

    def kernel(f_ref, c_ref, _, *refs):
        outs, later, sems = refs[:blocks], refs[blocks:-1], refs[-1]
        copies = [
            pltpu.make_async_copy(f_ref.at[1 + i // blocks, i % blocks, 0], later[i], sems.at[i])
            for i in range(2 * blocks)
        ]
        for copy in copies:
            copy.start()
        for b, out in enumerate(outs):
            out[...] = dot(f_ref[0, b, 0, :half], c_ref[b, 0]).astype(BF)
        for copy in copies:
            copy.wait()

    out = pl.pallas_call(
        kernel,
        in_specs=[VMEM] * 3,
        out_specs=[VMEM] * 3 * blocks,
        out_shape=[jax.ShapeDtypeStruct((half, cols), BF)] * blocks
        + [jax.ShapeDtypeStruct((rows, rows), BF)] * (2 * blocks),
        scratch_shapes=[pltpu.SemaphoreType.DMA((2 * blocks,))],
        compiler_params=SMALL,
        name="upper",
    )(factors, coefficients, after)
    return list(out[:blocks]), out[blocks : 2 * blocks], out[2 * blocks :]


def middle(weights, up, got, b, *after):
    half, cols = got.shape

    def kernel(f_ref, u_ref, g_ref, *refs):
        low_ref, up_ref = refs[len(after) :]
        w = f_ref
        u, g = u_ref[...], g_ref[...]
        low_ref[...] = (dot(w[half:, :half], u) + dot(w[half:, half:], g)).astype(BF)
        up_ref[...] = (dot(w[:half, :half], u) + dot(w[:half, half:], g)).astype(BF)

    return pl.pallas_call(
        kernel,
        in_specs=[VMEM] * (3 + len(after)),
        out_specs=[VMEM, VMEM],
        out_shape=[jax.ShapeDtypeStruct((half, cols), BF)] * 2,
        compiler_params=SMALL,
        name=f"middle{b}",
    )(weights, up, got, *after)


def last(weights, up, got, b, *after):
    half, cols = got.shape

    def kernel(f_ref, u_ref, g_ref, *refs):
        keep_ref, *gives = refs[len(after) :]
        step = half // len(gives)
        even = lax.rem(lax.axis_index("src"), 2) == 0
        w = f_ref
        u, g = u_ref[...], g_ref[...]
        out = (dot(w[:, :half], u) + dot(w[:, half:], g)).astype(BF)
        for i in range(2 * half // 32):
            one, two = out[i * 32 : i * 32 + 16], out[i * 32 + 16 : i * 32 + 32]
            keep_ref[i * 16 : i * 16 + 16] = jnp.where(even, one, two)
            at = i * 16 % step
            gives[i * 16 // step][at : at + 16] = jnp.where(even, two, one)

    return pl.pallas_call(
        kernel,
        in_specs=[VMEM] * (3 + len(after)),
        out_specs=[VMEM] * (1 + AP),
        out_shape=[jax.ShapeDtypeStruct((half, cols), BF)]
        + [jax.ShapeDtypeStruct((half // AP, cols), BF)] * AP,
        compiler_params=SMALL,
        name=f"last{b}",
    )(weights, up, got, *after)


def pack(keeps, backs):
    half, cols = keeps[0].shape
    n = len(keeps)
    piece = half // 8

    def kernel(*refs):
        kept, got, outs = refs[:n], refs[n : n * (1 + AP)], refs[n * (1 + AP) :]
        x = lax.axis_index("src") // 4
        for out, d in zip(outs, FLIPS):
            for b in range(n):
                for h in range(2):
                    row = h * half // 2
                    part = got[b * AP + row * AP // half]
                    at = pl.multiple_of((x ^ d) * piece, piece)
                    one = kept[b][pl.ds(row + at, piece)].astype(F32)
                    two = part[pl.ds(row % (half // AP) + at, piece)].astype(F32)
                    to = (b * 2 + h) * piece
                    out[to : to + piece] = (one + two).astype(BF)

    return pl.pallas_call(
        kernel,
        in_specs=[VMEM] * (n * (1 + AP)),
        out_specs=[VMEM] * 4,
        out_shape=[jax.ShapeDtypeStruct((n * 2 * piece, cols), BF)] * 4,
        compiler_params=SMALL,
        name="pack",
    )(*keeps, *[v for back in backs for v in back])


def shares(parts, outs, k):
    yh = lax.rem(lax.axis_index("src") // 2, 2)
    for b in range(parts[0].shape[0] // 64):
        for h, out in enumerate(outs):
            at = (b * 2 + h) * 32 + pl.multiple_of((yh ^ k) * 16, 16)
            one, two, three, four = [ref[pl.ds(at, 16)].astype(F32) for ref in parts]
            out[b * 16 : b * 16 + 16] = ((one + two) + (three + four)).astype(BF)


def split(parts):
    rows, cols = parts[0].shape
    rows //= 4

    def kernel(*refs):
        up_ref, low_ref, other_ref = refs[4:]
        shares(refs[:4], (up_ref, low_ref), 0)
        shares(refs[:4], (other_ref.at[:rows], other_ref.at[rows:]), 1)

    return pl.pallas_call(
        kernel,
        in_specs=[VMEM] * 4,
        out_specs=[VMEM] * 3,
        out_shape=[jax.ShapeDtypeStruct((n, cols), BF) for n in (rows, rows, 2 * rows)],
        compiler_params=SMALL,
        name="split",
    )(*parts)


def gather(parts, low, got):
    rows, cols = parts[0].shape
    rows //= 4

    def kernel(*refs):
        low_ref, got_ref, up_ref, up_other_ref, low_other_ref, send_ref = refs[4:]
        shares(refs[:4], (up_other_ref, low_other_ref), 1)
        shares(refs[:4], (up_ref, send_ref.at[:rows]), 0)
        both = low_ref[...].astype(F32) + got_ref[rows:].astype(F32)
        send_ref[rows:] = both.astype(BF)

    return pl.pallas_call(
        kernel,
        in_specs=[VMEM] * 6,
        out_specs=[VMEM] * 4,
        out_shape=[jax.ShapeDtypeStruct((n, cols), BF) for n in (rows, rows, rows, 2 * rows)],
        compiler_params=SMALL,
        name="gather",
    )(*parts, low, got)


def lows(one, two):
    rows, cols = one.shape

    def kernel(one_ref, two_ref, out_ref):
        out_ref[:rows] = two_ref[rows:].astype(F32)
        out_ref[rows:] = one_ref[...].astype(F32) + two_ref[:rows].astype(F32)

    return pl.pallas_call(
        kernel,
        in_specs=[VMEM] * 2,
        out_specs=VMEM,
        out_shape=jax.ShapeDtypeStruct((2 * rows, cols), F32),
        compiler_params=SMALL,
        name="lows",
    )(one, two)


def finish(early, late, low):
    rows, cols = low.shape
    blocks = rows // 16

    def kernel(*refs):
        ups, low_ref, out_ref = refs[:4], refs[4], refs[5]
        for b in range(blocks):
            one, two = ups[:2] if b < blocks // 2 else ups[2:]
            at = slice(b % (blocks // 2) * 16, b % (blocks // 2) * 16 + 16)
            out_ref[b, 0] = one[at].astype(F32) + two[at].astype(F32)
            out_ref[b, 1] = low_ref[b * 16 : b * 16 + 16]

    return pl.pallas_call(
        kernel,
        in_specs=[VMEM] * 5,
        out_specs=VMEM,
        out_shape=jax.ShapeDtypeStruct((blocks, 2, 16, cols), F32),
        compiler_params=SMALL,
        name="finish",
    )(*early, *late, low)


def solution(mesh):
    n_tgt, n_src = mesh.shape["tgt"], mesh.shape["src"]

    def swap(v, flip_tgt, flip_src):
        return lax.ppermute(v, AXES, moves(flip_tgt, flip_src, n_tgt, n_src))

    def local(coefficients, factors):
        blocks = coefficients.shape[0]
        low, token = opening(factors, coefficients)
        low = [low] + list(first(factors, coefficients, range(1, blocks), True, token))
        got = [swap(v, 1, 0) for v in low]
        up, second, third = rest(factors, coefficients, low[-1])
        keeps, backs = [None] * blocks, [None] * blocks
        order = up[0]

        def mix(b, *after):
            nonlocal order
            order, up[b] = middle(second[b], up[b], got[b], b, order, *after)
            got[b] = swap(order, 2, 0)

        def end(b, *after):
            nonlocal order
            keeps[b], *gives = last(third[b], up[b], got[b], b, order, *after)
            order = gives[0]
            backs[b] = [swap(v, 0, 1) for v in gives]

        def across(*group):
            own, *gives = pack([keeps[b] for b in group], [backs[b] for b in group])
            return [own] + [swap(v, 0, d * 4) for v, d in zip(gives, FLIPS[1:])]

        mix(0)
        mix(1)
        mix(2)
        end(0)
        mix(3)
        end(1)
        early = across(0, 1)
        end(2)
        end(3, early[1], early[2], early[3])
        late = across(2, 3)
        up, low, other = split(early)
        got = swap(other, 0, 2)
        late_up, up_other, low_other, send = gather(late, low, got)
        low = lows(swap(low_other, 4, 2), swap(send, 4, 0))
        return finish((up, got), (late_up, swap(up_other, 0, 2)), low)

    return jax.shard_map(
        local,
        mesh=mesh,
        in_specs=(P("tgt", "src", None, None), P(None, "tgt", "src", None, None)),
        out_specs=P("tgt", None, "src", None),
        check_vma=False,
    )
```

```python
import jax
import jax.numpy as jnp
from jax import lax
from jax.experimental import pallas as pl
from jax.experimental.pallas import tpu as pltpu
from jax.sharding import PartitionSpec as P

AXES = ("tgt", "src")
BF = jnp.bfloat16
F32 = jnp.float32
VMEM = pl.BlockSpec(memory_space=pltpu.VMEM)
ANY = pl.BlockSpec(memory_space=pl.ANY)
SMALL = pltpu.CompilerParams(vmem_limit_bytes=12 << 20)
AP = 2
FLIPS = (0, 2, 1, 3)
LARGE = pltpu.CompilerParams(vmem_limit_bytes=58 << 20)


def moves(flip_tgt, flip_src, n_tgt, n_src):
    return [
        (t * n_src + s, (t ^ flip_tgt) * n_src + (s ^ flip_src))
        for t in range(n_tgt)
        for s in range(n_src)
    ]


def dot(a, b):
    return jnp.dot(a, b, preferred_element_type=F32)


def opening(factors, coefficients):
    _, _, rows, cols = coefficients.shape
    half = rows // 2

    def kernel(f_hbm, c_hbm, o_ref, token_ref, f_ref, c_ref, sems):
        copies = [
            pltpu.make_async_copy(f_hbm.at[0, 0, 0, pl.ds(half, half)], f_ref, sems.at[0]),
            pltpu.make_async_copy(c_hbm.at[0, 0], c_ref, sems.at[1]),
        ]
        for copy in copies:
            copy.start()
        for copy in copies:
            copy.wait()
        o_ref[...] = dot(f_ref[...], c_ref[...]).astype(BF)
        token_ref[...] = c_ref[:16, :128]

    return pl.pallas_call(
        kernel,
        in_specs=[ANY, ANY],
        out_specs=[VMEM, VMEM],
        out_shape=[jax.ShapeDtypeStruct((half, cols), BF), jax.ShapeDtypeStruct((16, 128), BF)],
        scratch_shapes=[
            pltpu.VMEM((half, rows), BF),
            pltpu.VMEM((rows, cols), BF),
            pltpu.SemaphoreType.DMA((2,)),
        ],
        compiler_params=LARGE,
        name="opening",
    )(factors, coefficients)


def first(factors, coefficients, blocks, below, *after):
    _, _, rows, cols = coefficients.shape
    half = rows // 2
    top = half if below else 0

    def kernel(f_ref, c_ref, *refs):
        for b, out in zip(blocks, refs[len(after) :]):
            out[...] = dot(f_ref[0, b, 0, top : top + half], c_ref[b, 0]).astype(BF)

    return pl.pallas_call(
        kernel,
        in_specs=[VMEM] * (2 + len(after)),
        out_specs=[VMEM] * len(blocks),
        out_shape=[jax.ShapeDtypeStruct((half, cols), BF)] * len(blocks),
        compiler_params=SMALL,
        name="lower" if below else "upper",
    )(factors, coefficients, *after)


def rest(factors, coefficients, after):
    blocks, _, rows, cols = coefficients.shape
    half = rows // 2

    def kernel(f_ref, c_ref, _, *refs):
        outs, later, sems = refs[:blocks], refs[blocks:-1], refs[-1]
        copies = [
            pltpu.make_async_copy(f_ref.at[1 + i // blocks, i % blocks, 0], later[i], sems.at[i])
            for i in range(2 * blocks)
        ]
        for copy in copies:
            copy.start()
        for b, out in enumerate(outs):
            out[...] = dot(f_ref[0, b, 0, :half], c_ref[b, 0]).astype(BF)
        for copy in copies:
            copy.wait()

    out = pl.pallas_call(
        kernel,
        in_specs=[VMEM] * 3,
        out_specs=[VMEM] * 3 * blocks,
        out_shape=[jax.ShapeDtypeStruct((half, cols), BF)] * blocks
        + [jax.ShapeDtypeStruct((rows, rows), BF)] * (2 * blocks),
        scratch_shapes=[pltpu.SemaphoreType.DMA((2 * blocks,))],
        compiler_params=SMALL,
        name="upper",
    )(factors, coefficients, after)
    return list(out[:blocks]), out[blocks : 2 * blocks], out[2 * blocks :]


def middle(weights, up, got, b, *after):
    half, cols = got.shape

    def kernel(f_ref, u_ref, g_ref, *refs):
        low_ref, up_ref = refs[len(after) :]
        w = f_ref
        u, g = u_ref[...], g_ref[...]
        low_ref[...] = (dot(w[half:, :half], u) + dot(w[half:, half:], g)).astype(BF)
        up_ref[...] = (dot(w[:half, :half], u) + dot(w[:half, half:], g)).astype(BF)

    return pl.pallas_call(
        kernel,
        in_specs=[VMEM] * (3 + len(after)),
        out_specs=[VMEM, VMEM],
        out_shape=[jax.ShapeDtypeStruct((half, cols), BF)] * 2,
        compiler_params=SMALL,
        name=f"middle{b}",
    )(weights, up, got, *after)


def last(weights, up, got, b, *after):
    half, cols = got.shape

    def kernel(f_ref, u_ref, g_ref, *refs):
        keep_ref, *gives = refs[len(after) :]
        step = half // len(gives)
        even = lax.rem(lax.axis_index("src"), 2) == 0
        w = f_ref
        u, g = u_ref[...], g_ref[...]
        out = (dot(w[:, :half], u) + dot(w[:, half:], g)).astype(BF)
        for i in range(2 * half // 32):
            one, two = out[i * 32 : i * 32 + 16], out[i * 32 + 16 : i * 32 + 32]
            keep_ref[i * 16 : i * 16 + 16] = jnp.where(even, one, two)
            at = i * 16 % step
            gives[i * 16 // step][at : at + 16] = jnp.where(even, two, one)

    return pl.pallas_call(
        kernel,
        in_specs=[VMEM] * (3 + len(after)),
        out_specs=[VMEM] * (1 + AP),
        out_shape=[jax.ShapeDtypeStruct((half, cols), BF)]
        + [jax.ShapeDtypeStruct((half // AP, cols), BF)] * AP,
        compiler_params=SMALL,
        name=f"last{b}",
    )(weights, up, got, *after)


def pack(keeps, backs):
    half, cols = keeps[0].shape
    n = len(keeps)
    piece = half // 8

    def kernel(*refs):
        kept, got, outs = refs[:n], refs[n : n * (1 + AP)], refs[n * (1 + AP) :]
        x = lax.axis_index("src") // 4
        for out, d in zip(outs, FLIPS):
            for b in range(n):
                for h in range(2):
                    row = h * half // 2
                    part = got[b * AP + row * AP // half]
                    at = pl.multiple_of((x ^ d) * piece, piece)
                    one = kept[b][pl.ds(row + at, piece)].astype(F32)
                    two = part[pl.ds(row % (half // AP) + at, piece)].astype(F32)
                    to = (b * 2 + h) * piece
                    out[to : to + piece] = (one + two).astype(BF)

    return pl.pallas_call(
        kernel,
        in_specs=[VMEM] * (n * (1 + AP)),
        out_specs=[VMEM] * 4,
        out_shape=[jax.ShapeDtypeStruct((n * 2 * piece, cols), BF)] * 4,
        compiler_params=SMALL,
        name="pack",
    )(*keeps, *[v for back in backs for v in back])


def split(groups):
    n = len(groups)
    cols = groups[0][0].shape[1]
    counts = [group[0].shape[0] // 64 for group in groups]

    def kernel(*refs):
        ins, outs = refs[: 4 * n], refs[4 * n :]
        yh = lax.rem(lax.axis_index("src") // 2, 2)
        first = 0
        for g, count in enumerate(counts):
            for b in range(count):
                for h in range(2):
                    for k in range(2):
                        at = (b * 2 + h) * 32 + pl.multiple_of((yh ^ k) * 16, 16)
                        parts = [ref[pl.ds(at, 16)].astype(F32) for ref in ins[4 * g : 4 * g + 4]]
                        total = (parts[0] + parts[1]) + (parts[2] + parts[3])
                        to = (first + b) * 16
                        outs[2 * h + k][to : to + 16] = total.astype(BF)
            first += count

    return pl.pallas_call(
        kernel,
        in_specs=[VMEM] * (4 * n),
        out_specs=[VMEM] * 4,
        out_shape=[jax.ShapeDtypeStruct((16 * sum(counts), cols), BF)] * 4,
        compiler_params=SMALL,
        name="split",
    )(*[v for group in groups for v in group])


def lows(one, two):
    def kernel(one_ref, two_ref, out_ref):
        out_ref[...] = one_ref[...].astype(F32) + two_ref[...].astype(F32)

    return pl.pallas_call(
        kernel,
        in_specs=[VMEM] * 2,
        out_specs=VMEM,
        out_shape=jax.ShapeDtypeStruct(one.shape, F32),
        compiler_params=SMALL,
        name="lows",
    )(one, two)


def finish(up_one, up_two, low):
    rows, cols = low.shape
    blocks = rows // 16

    def kernel(one_ref, two_ref, low_ref, out_ref):
        for b in range(blocks):
            at = slice(b * 16, b * 16 + 16)
            out_ref[b, 0] = one_ref[at].astype(F32) + two_ref[at].astype(F32)
            out_ref[b, 1] = low_ref[at]

    return pl.pallas_call(
        kernel,
        in_specs=[VMEM] * 3,
        out_specs=VMEM,
        out_shape=jax.ShapeDtypeStruct((blocks, 2, 16, cols), F32),
        compiler_params=SMALL,
        name="finish",
    )(up_one, up_two, low)


def solution(mesh):
    n_tgt, n_src = mesh.shape["tgt"], mesh.shape["src"]

    def swap(v, flip_tgt, flip_src):
        return lax.ppermute(v, AXES, moves(flip_tgt, flip_src, n_tgt, n_src))

    def local(coefficients, factors):
        blocks = coefficients.shape[0]
        low, token = opening(factors, coefficients)
        low = [low] + list(first(factors, coefficients, range(1, blocks), True, token))
        got = [swap(v, 1, 0) for v in low]
        up, second, third = rest(factors, coefficients, low[-1])
        keeps, backs = [None] * blocks, [None] * blocks
        order = up[0]

        def mix(b, *after):
            nonlocal order
            order, up[b] = middle(second[b], up[b], got[b], b, order, *after)
            got[b] = swap(order, 2, 0)

        def end(b, *after):
            nonlocal order
            keeps[b], *gives = last(third[b], up[b], got[b], b, order, *after)
            order = gives[0]
            backs[b] = [swap(v, 0, 1) for v in gives]

        def across(*group):
            own, *gives = pack([keeps[b] for b in group], [backs[b] for b in group])
            return [own] + [swap(v, 0, d * 4) for v, d in zip(gives, FLIPS[1:])]

        mix(0)
        mix(1)
        mix(2)
        end(0)
        mix(3)
        end(1)
        early = across(0, 1)
        end(2)
        end(3, early[1], early[2], early[3])
        late = across(2, 3)
        up_mine, up_other, low_mine, low_other = split([early, late])
        low = lows(swap(low_other, 4, 2), swap(low_mine, 4, 0))
        return finish(up_mine, swap(up_other, 0, 2), low)

    return jax.shard_map(
        local,
        mesh=mesh,
        in_specs=(P("tgt", "src", None, None), P(None, "tgt", "src", None, None)),
        out_specs=P("tgt", None, "src", None),
        check_vma=False,
    )
```
